256 devices in a mesh: dp: 8 (over z), point: 32 (over x, y, core).
Axes of the slice: x: 4, y: 4, z: 8, core: 2. Of those that a mesh axis runs over, the one named last changes fastest.
Arguments:
- back_points: bfloat16 [8, 131072, 256], P('dp', 'point'), may hold values from -300 to 300
- fore_points: bfloat16 [8, 131072, 256], P('dp', 'point'), may hold values from -300 to 300
- cotangent: bfloat16 [8, 131072, 256], P('dp', 'point'), may hold values from -6 to 6
- w_value: bfloat16 [256, 256], replicated, may hold values from -0.375 to 0.375
- w_slice: bfloat16 [256, 512], replicated, may hold values from -1.09375 to 1.09375
- w_temp: bfloat16 [256, 8], replicated, may hold values from -0.375 to 0.375
- w_mix: float32 [256, 32], replicated, may hold values from -1 to 1
- w_out: bfloat16 [256, 256], replicated, may hold values from -0.375 to 0.375
Outputs:
- fore_result: bfloat16 [8, 131072, 256], P('dp', 'point')
- grad_points: bfloat16 [8, 131072, 256], P('dp', 'point')
- grad_value: float32 [256, 256], P('point')
- grad_slice: float32 [256, 512], P('point')
- grad_temp: float32 [256, 8], P('point')
- mixing_gradient: float32 [256, 32], P('point')
- grad_out: float32 [256, 256], P('point')
The draws below stay inside these ranges and needn't reach their ends.
All inputs are finite; a program needn't handle non-finite values.
Results may differ from the reference program's by a relative error of at most 0.007.
Values sent between devices are 32-bit elements; how exact they have to be, the bound alone decides.
No kernel may reach another device: no remote copies, remote signals or barrier semaphores. Data moves between devices by JAX's collectives and lax.ppermute only.
A program may use at most 128 MiB of HBM per device.

```python
import jax
import jax.numpy as jnp
from jax import lax

MODEL_WIDTH = 256
ATTENTION_HEADS = 8
HEAD_SIZE = 32
M = 64
POINTS = 131072
SAMPLES = 8


def textured(key, spread, peak):
    first, second = jax.random.split(key)
    base = jnp.clip(jax.random.normal(first, (SAMPLES, POINTS, MODEL_WIDTH), jnp.float32), -4.0, 4.0)
    position = jnp.arange(POINTS, dtype=jnp.float32) / POINTS
    rising = 1.0 + 2.0 * position
    factor = jnp.exp(jax.random.uniform(second, (SAMPLES, POINTS), jnp.float32) * jnp.log(spread))
    marked = jnp.arange(POINTS) % 509 == 7
    factor = jnp.where(marked[None, :], peak, factor)
    return (base * rising[None, :, None] * factor[:, :, None]).astype(jnp.bfloat16)


def draw_back_points(key, part):
    key = jax.random.fold_in(key, 11)
    return textured(key, 1.0, 1.0)


def draw_fore_points(key, part):
    key = jax.random.fold_in(key, 23)
    return textured(key, 1.0, 1.0)


def level_of(rng, extent, cuts, low, largest):
    def one(dim, parts):
        steps = jax.random.uniform(jax.random.fold_in(jax.random.fold_in(rng, 6), dim), (parts,), jnp.float32, low / len(cuts), largest / len(cuts))
        return jnp.repeat(jnp.exp(steps), extent[dim] // parts).reshape((-1,) + (1,) * (len(extent) - dim - 1))

    loudness = one(*cuts[0])
    for cut in cuts[1:]:
        loudness = loudness * one(*cut)
    return loudness


def gaussian(own_key, shape, scale, limit, pieces=(), held_as=jnp.bfloat16):
    array = scale * jax.random.normal(own_key, shape, jnp.float32)
    if pieces:
        array = array * level_of(own_key, shape, pieces, -0.22, 0.18)
    return jnp.clip(array, -limit, limit).astype(held_as)


def setup_inputs(seed: int = 0) -> dict:
    keys = jax.random.split(jax.random.key(seed), 9)
    back_points = draw_back_points(jax.random.fold_in(keys[8], 71), 0)
    fore_points = draw_fore_points(jax.random.fold_in(keys[8], 71), 0)
    cotangent = gaussian(keys[2], (SAMPLES, POINTS, MODEL_WIDTH), 1.0, 6.0, ((0, 8), (1, 32)))
    w_value = gaussian(keys[3], (MODEL_WIDTH, MODEL_WIDTH), MODEL_WIDTH ** -0.5, 0.375)
    w_slice = gaussian(keys[4], (MODEL_WIDTH, ATTENTION_HEADS * M), 0.19, 1.09375)
    w_temp = gaussian(keys[5], (MODEL_WIDTH, ATTENTION_HEADS), MODEL_WIDTH ** -0.5, 0.375)
    w_mix = gaussian(keys[6], (ATTENTION_HEADS * HEAD_SIZE, HEAD_SIZE), HEAD_SIZE ** -0.5, 1.0, (), jnp.float32)
    w_out = gaussian(keys[7], (MODEL_WIDTH, MODEL_WIDTH), MODEL_WIDTH ** -0.5, 0.375)
    return dict(back_points=back_points, fore_points=fore_points, cotangent=cotangent, w_value=w_value, w_slice=w_slice, w_temp=w_temp, w_mix=w_mix, w_out=w_out)


epsilon = 1e-5


def rounded_wide(values):
    narrow = lax.optimization_barrier(values.astype(jnp.bfloat16))
    return narrow.astype(jnp.float32)


def project(points, w_value, w_slice, w_temp):
    local_row_count = points.shape[0]
    values = jnp.dot(points, w_value, preferred_element_type=jnp.float32).astype(jnp.bfloat16)
    logits = jnp.dot(points, w_slice, preferred_element_type=jnp.float32).reshape(local_row_count, ATTENTION_HEADS, M)
    temp_coef = jnp.dot(points, w_temp, preferred_element_type=jnp.float32)
    temper = 0.5 + jax.nn.softplus(temp_coef)
    weights = jax.nn.softmax(logits / temper[:, :, None], axis=-1)
    return values, logits, temp_coef, temper, weights


def slice_side(values, weights, w_mix):
    local_row_count = values.shape[0]
    per_head_layout = values.reshape(local_row_count, ATTENTION_HEADS, HEAD_SIZE).astype(jnp.float32)
    full_weight_matrix = rounded_wide(weights)
    slice_numerator_sum = jnp.einsum('qij,qic->ijc', full_weight_matrix, per_head_layout)
    denominator = jnp.sum(weights, axis=0)
    token_rows = slice_numerator_sum / (denominator[:, :, None] + epsilon)
    block_list = w_mix.reshape(ATTENTION_HEADS, HEAD_SIZE, HEAD_SIZE)
    mixed_state = jnp.einsum('vuf,vfl->vul', token_rows, block_list, precision=lax.Precision.HIGHEST).astype(jnp.bfloat16)
    full_mixed_state = mixed_state.astype(jnp.float32)
    deslice_output = jnp.einsum('waf,aft->wat', full_weight_matrix, full_mixed_state).astype(jnp.bfloat16).reshape(local_row_count, MODEL_WIDTH)
    return per_head_layout, full_weight_matrix, denominator, token_rows, full_mixed_state, deslice_output


def reference(back_points, fore_points, cotangent, w_value, w_slice, w_temp, w_mix, w_out):
    block_list = w_mix.reshape(ATTENTION_HEADS, HEAD_SIZE, HEAD_SIZE)
    results = []
    point_grads = []
    grad_value = jnp.zeros((MODEL_WIDTH, MODEL_WIDTH), jnp.float32)
    grad_slice = jnp.zeros((MODEL_WIDTH, ATTENTION_HEADS * M), jnp.float32)
    grad_temp = jnp.zeros((MODEL_WIDTH, ATTENTION_HEADS), jnp.float32)
    mixing_gradient = jnp.zeros((ATTENTION_HEADS * HEAD_SIZE, HEAD_SIZE), jnp.float32)
    grad_out = jnp.zeros((MODEL_WIDTH, MODEL_WIDTH), jnp.float32)
    for sample in range(SAMPLES):
        fore_x = fore_points[sample]
        values, logits, temp_coef, temper, weights = project(fore_x, w_value, w_slice, w_temp)
        outcome = slice_side(values, weights, w_mix)
        results.append(jnp.dot(outcome[5], w_out, preferred_element_type=jnp.float32).astype(jnp.bfloat16))

        back_x = back_points[sample]
        local_row_count = back_x.shape[0]
        values, logits, temp_coef, temper, weights = project(back_x, w_value, w_slice, w_temp)
        per_head_layout, full_weight_matrix, denominator, token_rows, full_mixed_state, deslice_output = slice_side(values, weights, w_mix)
        cot = cotangent[sample]
        output_gradient = rounded_wide(jnp.dot(cot, w_out.T, preferred_element_type=jnp.float32)).reshape(local_row_count, ATTENTION_HEADS, HEAD_SIZE)
        mixed_state_gradient = jnp.einsum('qij,qic->ijc', full_weight_matrix, output_gradient)
        token_gradient = jnp.einsum('zbu,zgu->zbg', mixed_state_gradient, block_list, precision=lax.Precision.HIGHEST)
        inverse_denom = 1.0 / (denominator + epsilon)
        numerator_gradient = rounded_wide(token_gradient * inverse_denom[:, :, None])
        grad_denominator = -jnp.sum(token_gradient * token_rows, axis=-1) * inverse_denom
        weight_gradient = (jnp.einsum('ftu,tru->ftr', output_gradient, full_mixed_state)
                        + jnp.einsum('ftu,tru->ftr', per_head_layout, numerator_gradient)
                        + grad_denominator[None, :, :])
        grad_score = weights * (weight_gradient - jnp.sum(weights * weight_gradient, axis=-1, keepdims=True))
        grad_logits = (grad_score / temper[:, :, None]).reshape(local_row_count, ATTENTION_HEADS * M).astype(jnp.bfloat16)
        grad_coef = (-jax.nn.sigmoid(temp_coef) * jnp.sum(grad_score * logits, axis=-1) / (temper * temper)).astype(jnp.bfloat16)
        value_gradient = jnp.einsum('waf,aft->wat', full_weight_matrix, numerator_gradient).astype(jnp.bfloat16).reshape(local_row_count, MODEL_WIDTH)
        total = (jnp.dot(value_gradient, w_value.T, preferred_element_type=jnp.float32)
                 + jnp.dot(grad_logits, w_slice.T, preferred_element_type=jnp.float32)
                 + jnp.dot(grad_coef, w_temp.T, preferred_element_type=jnp.float32))
        point_grads.append(total.astype(jnp.bfloat16))
        grad_value = grad_value + jnp.dot(back_x.T, value_gradient, preferred_element_type=jnp.float32)
        grad_slice = grad_slice + jnp.dot(back_x.T, grad_logits, preferred_element_type=jnp.float32)
        grad_temp = grad_temp + jnp.dot(back_x.T, grad_coef, preferred_element_type=jnp.float32)
        grad_out = grad_out + jnp.dot(deslice_output.T, cot, preferred_element_type=jnp.float32)
        mixing_gradient = mixing_gradient + jnp.einsum('pyk,pyz->pkz', token_rows, mixed_state_gradient, precision=lax.Precision.HIGHEST).reshape(ATTENTION_HEADS * HEAD_SIZE, HEAD_SIZE)
    return (jnp.stack(results), jnp.stack(point_grads), grad_value, grad_slice, grad_temp, mixing_gradient, grad_out)
```

```python
import jax
import jax.numpy as jnp
from jax import lax
from jax.sharding import PartitionSpec as P

MODEL_WIDTH = 256
ATTENTION_HEADS = 8
HEAD_SIZE = 32
M = 64


epsilon = 1e-05

CORE_SWAP = [(i, i ^ 1) for i in range(32)]


def along_x(step):
    return [(i, (i + 8 * step) % 32) for i in range(32)]


def along_y(step):
    return [(i, i // 8 * 8 + (i + 2 * step) % 8) for i in range(32)]


def core_halves(block, first, second):
    core = lax.axis_index("point") % 2
    own = jnp.where(core == 0, first, second)
    other = jnp.where(core == 0, second, first)
    return own + lax.ppermute(other, "point", CORE_SWAP)


def point_all_reduce(arrays, rows):
    flat = jnp.concatenate([a.reshape(-1) for a in arrays])
    flat = jnp.pad(flat, (0, rows * 128 - flat.size)).reshape(rows, 128)
    half = core_halves(flat, flat[: rows // 2], flat[rows // 2 :])
    for ring in (along_x, along_y):
        parts = [lax.ppermute(half, "point", ring(step)) for step in (1, 2, 3)]
        half = half + parts[0] + parts[1] + parts[2]
    other = lax.ppermute(half, "point", CORE_SWAP)
    core = lax.axis_index("point") % 2
    flat = jnp.concatenate(
        [jnp.where(core == 0, half, other), jnp.where(core == 0, other, half)]
    ).reshape(-1)
    out = []
    for a in arrays:
        out.append(flat[: a.size].reshape(a.shape))
        flat = flat[a.size :]
    return out


def point_reduce_scatter(wide):
    blocks = wide.reshape(16, 2, 8, wide.shape[1])
    half = core_halves(blocks, blocks[:, 0], blocks[:, 1])
    groups = [[i for i in range(32) if i % 2 == core] for core in range(2)]
    return lax.all_to_all(half, "point", 0, 0, axis_index_groups=groups).sum(0)


def sample_all_reduce(rows):
    copies = jnp.broadcast_to(rows[None], (8,) + rows.shape)
    return lax.all_to_all(copies, "dp", 0, 0).sum(0)


def project(points, w_value, w_slice, w_temp):
    local_row_count = points.shape[0]
    values = jnp.dot(points, w_value, preferred_element_type=jnp.float32).astype(jnp.bfloat16)
    logits = jnp.dot(points, w_slice, preferred_element_type=jnp.float32).reshape(
        local_row_count, ATTENTION_HEADS, M
    )
    temp_coef = jnp.dot(points, w_temp, preferred_element_type=jnp.float32)
    temper = 0.5 + jax.nn.softplus(temp_coef)
    weights = jax.nn.softmax(logits / temper[:, :, None], axis=-1)
    return (
        values.reshape(local_row_count, ATTENTION_HEADS, HEAD_SIZE),
        logits,
        temp_coef,
        temper,
        weights,
        weights.astype(jnp.bfloat16),
    )


def local_sums(per_head_layout, weights, narrow_weight_part):
    slice_numerator_sum = jnp.einsum(
        "qij,qic->ijc", narrow_weight_part, per_head_layout, preferred_element_type=jnp.float32
    )
    return (slice_numerator_sum, jnp.sum(weights, axis=0))


def slice_tokens(slice_numerator_sum, denominator, block_list):
    token_rows = slice_numerator_sum / (denominator[:, :, None] + epsilon)
    mixed_state = jnp.einsum(
        "vuf,vfl->vul", token_rows, block_list, precision=lax.Precision.HIGHEST
    ).astype(jnp.bfloat16)
    return (token_rows, mixed_state)


def deslice(narrow_weight_part, mixed_state):
    local_row_count = narrow_weight_part.shape[0]
    heads_out = jnp.einsum(
        "waf,aft->wat", narrow_weight_part, mixed_state, preferred_element_type=jnp.float32
    )
    return heads_out.astype(jnp.bfloat16).reshape(local_row_count, MODEL_WIDTH)


def contract_rows(left, right):
    return lax.dot_general(
        left, right, (((0,), (0,)), ((), ())), preferred_element_type=jnp.float32
    )


def local(back_points, fore_points, cotangent, w_value, w_slice, w_temp, w_mix, w_out):
    block_list = w_mix.reshape(ATTENTION_HEADS, HEAD_SIZE, HEAD_SIZE)
    fore_x = fore_points[0]
    back_x = back_points[0]
    cot = cotangent[0]
    local_row_count = back_x.shape[0]
    fore_heads, fore_logits, fore_coef, fore_temper, fore_weights, fore_narrow = project(
        fore_x, w_value, w_slice, w_temp
    )
    fore_numer, fore_denom = local_sums(fore_heads, fore_weights, fore_narrow)
    backward_head_split, logits, temp_coef, temper, weights, backward_narrow_part = project(
        back_x, w_value, w_slice, w_temp
    )
    back_numer, back_denom = local_sums(backward_head_split, weights, backward_narrow_part)
    output_gradient = (
        jnp.dot(cot, w_out.T, preferred_element_type=jnp.float32)
        .astype(jnp.bfloat16)
        .reshape(local_row_count, ATTENTION_HEADS, HEAD_SIZE)
    )
    local_mixed_state = jnp.einsum(
        "qij,qic->ijc", backward_narrow_part, output_gradient, preferred_element_type=jnp.float32
    )
    back_sums = point_all_reduce([back_numer, local_mixed_state, back_denom], 272)
    back_numer, mixed_state_gradient, back_denom = back_sums
    fore_numer, fore_denom = point_all_reduce([fore_numer, fore_denom], 144)
    fore_tokens, fore_mixed = slice_tokens(fore_numer, fore_denom, block_list)
    fore_desliced = deslice(fore_narrow, fore_mixed)
    fore_result = jnp.dot(fore_desliced, w_out, preferred_element_type=jnp.float32).astype(
        jnp.bfloat16
    )
    token_rows, mixed_state = slice_tokens(back_numer, back_denom, block_list)
    deslice_output = deslice(backward_narrow_part, mixed_state)
    mix_term = jnp.einsum(
        "pyk,pyz->pkz", token_rows, mixed_state_gradient, precision=lax.Precision.HIGHEST
    ).reshape(ATTENTION_HEADS * HEAD_SIZE, HEAD_SIZE)
    token_gradient = jnp.einsum(
        "zbu,zgu->zbg", mixed_state_gradient, block_list, precision=lax.Precision.HIGHEST
    )
    inverse_denom = 1.0 / (back_denom + epsilon)
    numerator_gradient = (token_gradient * inverse_denom[:, :, None]).astype(jnp.bfloat16)
    grad_denominator = -jnp.sum(token_gradient * token_rows, axis=-1) * inverse_denom
    weight_gradient = (
        jnp.einsum("ftu,tru->ftr", output_gradient, mixed_state, preferred_element_type=jnp.float32)
        + jnp.einsum(
            "ftu,tru->ftr",
            backward_head_split,
            numerator_gradient,
            preferred_element_type=jnp.float32,
        )
        + grad_denominator[None, :, :]
    )
    grad_score = weights * (
        weight_gradient - jnp.sum(weights * weight_gradient, axis=-1, keepdims=True)
    )
    grad_logits = (
        (grad_score / temper[:, :, None])
        .reshape(local_row_count, ATTENTION_HEADS * M)
        .astype(jnp.bfloat16)
    )
    grad_coef = (
        -jax.nn.sigmoid(temp_coef) * jnp.sum(grad_score * logits, axis=-1) / (temper * temper)
    ).astype(jnp.bfloat16)
    value_gradient = jnp.einsum(
        "waf,aft->wat", backward_narrow_part, numerator_gradient, preferred_element_type=jnp.float32
    )
    value_gradient = value_gradient.astype(jnp.bfloat16).reshape(local_row_count, MODEL_WIDTH)
    total = (
        jnp.dot(value_gradient, w_value.T, preferred_element_type=jnp.float32)
        + jnp.dot(grad_logits, w_slice.T, preferred_element_type=jnp.float32)
        + jnp.dot(grad_coef, w_temp.T, preferred_element_type=jnp.float32)
    )
    grad_points = total.astype(jnp.bfloat16)
    value_term = contract_rows(back_x, value_gradient)
    slice_term = contract_rows(back_x, grad_logits)
    temp_term = contract_rows(back_x, grad_coef)
    out_term = contract_rows(deslice_output, cot)
    own_mix = lax.dynamic_slice_in_dim(mix_term, lax.axis_index("point") * 8, 8, 0)
    wide = jnp.concatenate(
        [value_term, slice_term, out_term, jnp.pad(temp_term, ((0, 0), (0, 120)))], axis=1
    )
    rows = point_reduce_scatter(wide)
    rows = sample_all_reduce(rows + jnp.pad(own_mix, ((0, 0), (1032, 88))))
    return (
        fore_result[None],
        grad_points[None],
        rows[:, :256],
        rows[:, 256:768],
        rows[:, 1024:1032],
        rows[:, 1032:1064],
        rows[:, 768:1024],
    )


def solution(mesh):
    in_specs = (
        P("dp", "point", None),
        P("dp", "point", None),
        P("dp", "point", None),
        P(),
        P(),
        P(),
        P(),
        P(),
    )
    out_specs = (
        P("dp", "point", None),
        P("dp", "point", None),
        P("point", None),
        P("point", None),
        P("point", None),
        P("point", None),
        P("point", None),
    )
    return jax.shard_map(local, mesh=mesh, in_specs=in_specs, out_specs=out_specs, check_vma=False)
```

```python
import functools

import jax
import jax.numpy as jnp
from jax import lax
from jax.experimental import pallas as pl
from jax.experimental.pallas import tpu as pltpu
from jax.sharding import PartitionSpec as P

MODEL_WIDTH = 256
ATTENTION_HEADS = 8
HEAD_SIZE = 32
M = 64
TILE = 2048
FIRST_TILE = 1024
GRAD_TILE = 1024
SUB = 512
LOG2_E = 1.4426950408889634
VMEM_LIMIT = 24 * 1024 * 1024


epsilon = 1e-05

CORE_SWAP = [(i, i ^ 1) for i in range(32)]


def along_x(flip):
    return [(i, i ^ (8 * flip)) for i in range(32)]


def along_y(flip):
    return [(i, i ^ (2 * flip)) for i in range(32)]


def core_halves(block, first, second):
    core = lax.axis_index("point") % 2
    own = jnp.where(core == 0, first, second)
    other = jnp.where(core == 0, second, first)
    return own + lax.ppermute(other, "point", CORE_SWAP)


def row_halves(flat):
    rows = flat.shape[0] // 2
    return core_halves(flat, flat[:rows], flat[rows:])


def pair_sum(half, pairs):
    return half + lax.ppermute(half, "point", pairs)


def quad_sum(half, pairs):
    parts = [lax.ppermute(half, "point", pairs(flip)) for flip in (1, 3, 2)]
    return half + parts[0] + parts[1] + parts[2]


def both_halves(half):
    other = lax.ppermute(half, "point", CORE_SWAP)
    core = lax.axis_index("point") % 2
    return jnp.concatenate(
        [jnp.where(core == 0, half, other), jnp.where(core == 0, other, half)]
    )


def tie(*arrays):
    return lax.optimization_barrier(arrays)


def dot_nt(left, right):
    return lax.dot_general(
        left, right, (((1,), (1,)), ((), ())), preferred_element_type=jnp.float32
    )


def dot_nn(left, right):
    return jnp.dot(left, right, preferred_element_type=jnp.float32)


def dot_exact(left, right, dims):
    return lax.dot_general(
        left,
        right,
        ((dims, ((), ()))),
        precision=lax.Precision.HIGHEST,
        preferred_element_type=jnp.float32,
    )


def transpose_weights(wt, w_slice, w_value, w_temp):
    wt[0:512, :] = w_slice[...].T
    wt[512:768, :] = w_value[...].T
    wt[768:784, :] = padded_temp(w_temp).astype(jnp.bfloat16)


def padded_temp(w_temp):
    return jnp.concatenate(
        [w_temp[...].astype(jnp.float32), jnp.zeros((8, MODEL_WIDTH), jnp.float32)], axis=0
    )


def head_rows(h, size):
    return slice(h * size, (h + 1) * size)


def temper_of(coef):
    return 0.5 + jnp.maximum(coef, 0.0) + jnp.log1p(jnp.exp(-jnp.abs(coef)))


def lane_sum(w):
    total = w[:, 0:128]
    for k in range(1, w.shape[1] // 128):
        total = total + w[:, k * 128 : (k + 1) * 128]
    return total


def head_weights(logits, scale, wb, den, stats, h, columns, where=None):
    top = jnp.max(logits, axis=0, keepdims=True)
    e = jnp.exp2((logits - top) * scale)
    inv = 1.0 / jnp.sum(e, axis=0, keepdims=True)
    w = e * inv
    wb[head_rows(h, M), columns] = w.astype(jnp.bfloat16)
    den[head_rows(h, M), :] += lane_sum(w)
    if stats is not None:
        stats[h : h + 1, where] = top
        stats[8 + h : 9 + h, where] = inv


def pack_denominators(den):
    columns = [
        jnp.sum(den[head_rows(h, M), :], axis=1, keepdims=True) for h in range(ATTENTION_HEADS)
    ]
    lane = lax.broadcasted_iota(jnp.int32, (M, 128), 1)
    wide = jnp.zeros((M, 128), jnp.float32)
    for h in range(ATTENTION_HEADS):
        wide = jnp.where(lane == h, columns[h], wide)
    return jnp.concatenate(
        [wide.T[:8, :], jnp.zeros((8, M), jnp.float32)], axis=0
    )


def inverse_denominators(rows):
    tall = jnp.concatenate(
        [
            jnp.concatenate([rows, jnp.zeros((8, 128 - M), jnp.float32)], axis=1),
            jnp.zeros((120, 128), jnp.float32),
        ],
        axis=0,
    ).T
    inverse = 1.0 / (tall[:M, :] + epsilon)
    return [inverse[:, h : h + 1] for h in range(ATTENTION_HEADS)]


def back_sums_kernel(
    x_ref, cot_ref, ws_ref, wv_ref, wt_ref, wo_ref,
    sums_ref, vo_ref, stats_ref, weights_ref,
    wb, den, acc,
):
    step = pl.program_id(0)

    @pl.when(step == 0)
    def _():
        transpose_weights(weights_ref, ws_ref, wv_ref, wt_ref)
        den[...] = jnp.zeros_like(den)
        acc[...] = jnp.zeros_like(acc)

    for part in range(FIRST_TILE // SUB):
        columns = slice(part * SUB, (part + 1) * SUB)
        where = pl.ds(pl.multiple_of(step * FIRST_TILE + part * SUB, SUB), SUB)
        x = x_ref[columns, :]
        projected = dot_nt(weights_ref[...], x)
        values = projected[512:768, :].astype(jnp.bfloat16)
        out_grad = dot_nt(wo_ref[...], cot_ref[columns, :]).astype(jnp.bfloat16)
        coef = projected[768:776, :]
        inv_temper = 1.0 / temper_of(coef)
        stats_ref[16:24, where] = inv_temper
        stats_ref[24:32, where] = coef
        scale = inv_temper * LOG2_E
        for g in range(2):
            mixed_rows = []
            for j in range(4):
                h = g * 4 + j
                mixed_rows += [
                    values[head_rows(h, HEAD_SIZE), :], out_grad[head_rows(h, HEAD_SIZE), :]
                ]
                head_weights(
                    projected[head_rows(h, M), :], scale[h : h + 1, :], wb, den, stats_ref, h, columns, where
                )
            vo_ref[g * 256 : (g + 1) * 256, where] = jnp.concatenate(mixed_rows, axis=0)
    tile = pl.ds(pl.multiple_of(step * FIRST_TILE, FIRST_TILE), FIRST_TILE)
    for g in range(2):
        rows = slice(g * 256, (g + 1) * 256)
        acc[g, :, :] += dot_nt(wb[rows, :], vo_ref[rows, tile])

    @pl.when(step == pl.num_programs(0) - 1)
    def _():
        lane = lax.broadcasted_iota(jnp.int32, (M, 128), 1)
        for q in range(4):
            g, p = q // 2, q % 2
            columns = slice(128 * p, 128 * p + 128)
            even = acc[g, 128 * p : 128 * p + 64, columns]
            odd = acc[g, 128 * p + 64 : 128 * p + 128, columns]
            sums_ref[q * M : (q + 1) * M, :] = jnp.where(lane < 64, even, odd)
        sums_ref[256:272, :] = jnp.zeros((16, 128), jnp.float32)
        sums_ref[256:272, 0:M] = pack_denominators(den)


def fore_sums_kernel(x_ref, weights_ref, before_ref, *refs):
    sums_ref, wb, den, acc, values = refs[-5:]
    step = pl.program_id(0)

    @pl.when(step == 0)
    def _():
        den[...] = jnp.zeros_like(den)
        acc[...] = jnp.zeros_like(acc)

    for part in range(TILE // SUB):
        columns = slice(part * SUB, (part + 1) * SUB)
        projected = dot_nt(weights_ref[...], x_ref[columns, :])
        values[:, columns] = projected[512:768, :].astype(jnp.bfloat16)
        scale = LOG2_E / temper_of(projected[768:776, :])
        for h in range(ATTENTION_HEADS):
            head_weights(
                projected[head_rows(h, M), :], scale[h : h + 1, :], wb, den, None, h, columns
            )
    for g in range(2):
        acc[g, :, :] += dot_nt(
            wb[g * 256 : (g + 1) * 256, :], values[g * 128 : (g + 1) * 128, :]
        )

    @pl.when(step == pl.num_programs(0) - 1)
    def _():
        lane = lax.broadcasted_iota(jnp.int32, (M, 128), 1)
        for g in range(2):
            block = acc[g, 0:M, :]
            for j in range(1, 4):
                block = jnp.where(lane // HEAD_SIZE == j, acc[g, head_rows(j, M), :], block)
            rows = slice(g * M, (g + 1) * M)
            sums_ref[rows, :] = block + before_ref[rows, :]
        sums_ref[128:144, :] = jnp.zeros((16, 128), jnp.float32)
        sums_ref[128:144, 0:M] = pack_denominators(den) + before_ref[128:144, 0:M]


def back_grads_kernel(
    sums_ref, mix_ref, x_ref, cot_ref, weights_ref, vo_ref, stats_ref,
    wide_ref, gram_ref, stack_ref,
    blocks, blocks_t, shift, wb, des, dots, grads, grad_out,
):
    step = pl.program_id(0)

    @pl.when(step == 0)
    def _():
        grads[...] = jnp.zeros_like(grads)
        grad_out[...] = jnp.zeros_like(grad_out)
        blocks[...] = jnp.zeros_like(blocks)
        lane = lax.broadcasted_iota(jnp.int32, (M, 128), 1)
        first = lane % 64 < HEAD_SIZE
        inverse = inverse_denominators(sums_ref[256:264, 0:M])
        for q in range(4):
            g, p = q // 2, q % 2
            scale = jnp.where(lane < 64, inverse[2 * q], inverse[2 * q + 1])
            scaled = sums_ref[q * M : (q + 1) * M, :] * jnp.where(first, scale, 1.0)
            gram_ref[q * 128 : (q + 1) * 128, :] = dot_exact(scaled, scaled, ((0,), (0,)))
            mapped = dot_exact(scaled, mix_ref[q * 128 : (q + 1) * 128, :], ((1,), (0,)))
            product = jnp.where(first, mapped * scaled, 0.0)
            block = mapped * jnp.where(first, scale, 1.0)
            for e in range(2):
                h = 2 * q + e
                own = (lane // 64) == e
                rows = slice((h % 4) * M, (h % 4 + 1) * M)
                columns = slice(128 * p, 128 * p + 128)
                blocks[g, rows, columns] = jnp.where(own, block, 0.0).astype(jnp.bfloat16)
                gd = -jnp.sum(jnp.where(own, product, 0.0), axis=1, keepdims=True) * inverse[h]
                shift[head_rows(h, M), :] = jnp.broadcast_to(gd, (M, 128))
        for g in range(2):
            blocks_t[g, :, :] = blocks[g, :, :].T

    for part in range(GRAD_TILE // SUB):
        columns = slice(part * SUB, (part + 1) * SUB)
        where = pl.ds(pl.multiple_of(step * GRAD_TILE + part * SUB, SUB), SUB)
        logits = dot_nt(weights_ref[0:512, :], x_ref[columns, :])
        for g in range(2):
            rows = slice(g * 256, (g + 1) * 256)
            grad_w = dot_nn(blocks[g, :, :], vo_ref[rows, where])
            for j in range(4):
                h = g * 4 + j
                inv_temper = stats_ref[16 + h : 17 + h, where]
                t = logits[head_rows(h, M), :] - stats_ref[h : h + 1, where]
                w = jnp.exp2(t * (inv_temper * LOG2_E)) * stats_ref[8 + h : 9 + h, where]
                wb[head_rows(h, M), columns] = w.astype(jnp.bfloat16)
                gd = shift[head_rows(h, M), :]
                gw = grad_w[head_rows(j, M), :] + jnp.concatenate([gd] * (SUB // 128), axis=1)
                inner = jnp.sum(w * gw, axis=0, keepdims=True)
                score = w * (gw - inner)
                dots[h : h + 1, columns] = jnp.sum(score * t, axis=0, keepdims=True)
                stack_ref[head_rows(h, M), columns] = (score * inv_temper).astype(jnp.bfloat16)
    for g in range(2):
        rows = slice(g * 256, (g + 1) * 256)
        both = dot_nn(blocks_t[g, :, :], wb[rows, :]).astype(jnp.bfloat16)
        for j in range(4):
            h = g * 4 + j
            stack_ref[512 + h * 32 : 544 + h * 32, :] = both[j * 64 : j * 64 + 32, :]
            des[head_rows(h, HEAD_SIZE), :] = both[j * 64 + 32 : j * 64 + 64, :]
    tile = pl.ds(pl.multiple_of(step * GRAD_TILE, GRAD_TILE), GRAD_TILE)
    inv_temper = stats_ref[16:24, tile]
    coef = stats_ref[24:32, tile]
    grad_coef = -jax.nn.sigmoid(coef) * dots[...] * (inv_temper * inv_temper)
    stack_ref[768:784, :] = jnp.concatenate(
        [grad_coef, jnp.zeros_like(grad_coef)], axis=0
    ).astype(jnp.bfloat16)
    grads[...] += dot_nn(stack_ref[...], x_ref[...])
    grad_out[...] += dot_nn(des[...], cot_ref[...])

    @pl.when(step == pl.num_programs(0) - 1)
    def _():
        wide_ref[:, 0:256] = grads[512:768, :].T
        wide_ref[:, 256:768] = grads[0:512, :].T
        wide_ref[:, 768:1024] = grad_out[...]
        wide_ref[:, 1024:1152] = jnp.concatenate(
            [grads[768:784, :], jnp.zeros((112, MODEL_WIDTH), jnp.float32)], axis=0
        ).T


def grad_points_kernel(stack_ref, ws_ref, wv_ref, wt_ref, out_ref, wide):
    @pl.when(pl.program_id(0) == 0)
    def _():
        wide[:, 0:512] = ws_ref[...]
        wide[:, 512:768] = wv_ref[...]
        wide[:, 768:784] = padded_temp(wt_ref).T.astype(jnp.bfloat16)

    out_ref[...] = dot_nn(wide[...], stack_ref[...]).T.astype(jnp.bfloat16)


def fore_result_kernel(sums_ref, mix_ref, wb_ref, wo_ref, out_ref, blocks_t, wo_t):
    @pl.when(pl.program_id(0) == 0)
    def _():
        wo_t[...] = wo_ref[...].T
        lane = lax.broadcasted_iota(jnp.int32, (M, 128), 1)
        inverse = inverse_denominators(sums_ref[128:136, 0:M])
        for g in range(2):
            scale = jnp.zeros((M, 128), jnp.float32)
            for j in range(4):
                scale = jnp.where(lane // HEAD_SIZE == j, inverse[g * 4 + j], scale)
            tokens = sums_ref[g * M : (g + 1) * M, :] * scale
            mixed = dot_exact(tokens, mix_ref[g * 128 : (g + 1) * 128, :], ((1,), (0,)))
            rows = [jnp.where(lane // HEAD_SIZE == j, mixed, 0.0) for j in range(4)]
            blocks_t[g, :, :] = jnp.concatenate(rows, axis=0).T.astype(jnp.bfloat16)

    parts = [
        dot_nn(blocks_t[g, :, :], wb_ref[g * 256 : (g + 1) * 256, :]).astype(jnp.bfloat16)
        for g in range(2)
    ]
    out = dot_nn(wo_t[...], jnp.concatenate(parts, axis=0))
    out_ref[...] = out.T.astype(jnp.bfloat16)


def f32(*shape):
    return jax.ShapeDtypeStruct(shape, jnp.float32)


def bf16(*shape):
    return jax.ShapeDtypeStruct(shape, jnp.bfloat16)


def near(*shape, dtype=jnp.bfloat16):
    return pltpu.VMEM(shape, dtype)


def rows_of(tile, width, first=0):
    return pl.BlockSpec((tile, width), lambda i: (i + first, 0))


def columns_of(tile, rows, first=0):
    return pl.BlockSpec((rows, tile), lambda i: (0, i + first))


def whole(*shape):
    return pl.BlockSpec(shape, lambda i: (0,) * len(shape))


NEAR = pl.BlockSpec(memory_space=pltpu.VMEM)


def call(kernel, points, tile, inputs, outputs, scratch, macs, moved, aliases={}):
    operands = [
        a if spec is NEAR else pltpu.with_memory_space_constraint(a, pltpu.HBM)
        for a, spec in inputs
    ]
    return pl.pallas_call(
        kernel,
        grid=(points // tile,),
        in_specs=[spec for _, spec in inputs],
        out_specs=[spec for _, spec in outputs],
        out_shape=[shape for shape, _ in outputs],
        scratch_shapes=scratch,
        input_output_aliases=aliases,
        compiler_params=pltpu.CompilerParams(vmem_limit_bytes=VMEM_LIMIT),
        cost_estimate=pl.CostEstimate(
            flops=2 * macs * points, bytes_accessed=moved * points, transcendentals=0
        ),
    )(*operands)


def back_sums(x, cot, w_slice, w_value, w_temp, w_out):
    points = x.shape[0]
    return call(
        back_sums_kernel,
        points,
        FIRST_TILE,
        [(x, rows_of(FIRST_TILE, 256)), (cot, rows_of(FIRST_TILE, 256)),
         (w_slice, whole(256, 512)), (w_value, whole(256, 256)), (w_temp, whole(8, 256)),
         (w_out, whole(256, 256))],
        [(f32(272, 128), NEAR), (near(512, points), NEAR),
         (near(32, points, dtype=jnp.float32), NEAR), (near(784, 256), NEAR)],
        [pltpu.VMEM((512, FIRST_TILE), jnp.bfloat16), pltpu.VMEM((512, 128), jnp.float32),
         pltpu.VMEM((2, 256, 256), jnp.float32)],
        600_000,
        2200,
    )


def fore_sums(x, weights, before, wb, first, tiles):
    points = x.shape[0]
    earlier = [] if wb is None else [(wb, pl.BlockSpec(memory_space=pl.ANY))]
    return call(
        fore_sums_kernel,
        tiles * TILE,
        TILE,
        [(x, rows_of(TILE, 256, first)), (weights, NEAR), (before, NEAR)] + earlier,
        [(f32(144, 128), NEAR), (pltpu.HBM((512, points), jnp.bfloat16), columns_of(TILE, 512, first))],
        [pltpu.VMEM((512, 128), jnp.float32), pltpu.VMEM((2, 256, 128), jnp.float32),
         pltpu.VMEM((256, TILE), jnp.bfloat16)],
        500_000,
        1500,
        {} if wb is None else {3: 1},
    )


def back_grads(sums, mix, x, cot, weights, vo, stats):
    points = x.shape[0]
    tile = GRAD_TILE
    return call(
        back_grads_kernel,
        points,
        tile,
        [(sums, NEAR), (mix, NEAR), (x, rows_of(tile, 256)), (cot, rows_of(tile, 256)),
         (weights, NEAR), (vo, NEAR), (stats, NEAR)],
        [(f32(256, 1152), NEAR), (f32(512, 128), NEAR), (pltpu.HBM((784, points), jnp.bfloat16), columns_of(tile, 784))],
        [pltpu.VMEM((2, 256, 256), jnp.bfloat16), pltpu.VMEM((2, 256, 256), jnp.bfloat16),
         pltpu.VMEM((512, 128), jnp.float32), pltpu.VMEM((512, tile), jnp.bfloat16),
         pltpu.VMEM((256, tile), jnp.bfloat16), pltpu.VMEM((8, tile), jnp.float32),
         pltpu.VMEM((784, 256), jnp.float32), pltpu.VMEM((256, 256), jnp.float32)],
        800_000,
        3800,
    )


def grad_of_points(stack, w_slice, w_value, w_temp):
    points = stack.shape[1]
    return call(
        grad_points_kernel,
        points,
        TILE,
        [(stack, columns_of(TILE, 784)), (w_slice, whole(256, 512)), (w_value, whole(256, 256)),
         (w_temp, whole(8, 256))],
        [(bf16(points, 256), rows_of(TILE, 256))],
        [pltpu.VMEM((256, 784), jnp.bfloat16)],
        200_000,
        2100,
    )[0]


def fore_results(sums, mix, wb, w_out):
    points = wb.shape[1]
    return call(
        fore_result_kernel,
        points,
        TILE,
        [(sums, NEAR), (mix, NEAR), (wb, columns_of(TILE, 512)), (w_out, whole(256, 256))],
        [(bf16(points, 256), rows_of(TILE, 256))],
        [pltpu.VMEM((2, 128, 256), jnp.bfloat16), pltpu.VMEM((256, 256), jnp.bfloat16)],
        130_000,
        1600,
    )[0]


def one_hot(rows, columns, hit):
    r = lax.broadcasted_iota(jnp.int32, (rows, columns), 0)
    c = lax.broadcasted_iota(jnp.int32, (rows, columns), 1)
    return jnp.where(hit(r, c), 1.0, 0.0)


def mix_maps_kernel(turned_ref, back_ref, fore_ref):
    turned = jnp.concatenate([turned_ref[...]] * 4, axis=0)
    spread = one_hot(128, 128, lambda r, c: (r // 32 == c // 64) & (r % 32 + 32 == c % 64))
    spread_first = one_hot(128, 128, lambda r, c: (r // 32 == c // 64) & (r % 32 == c % 64))
    same = one_hot(128, 128, lambda r, c: r // 32 == c // 32)
    for g in range(2):
        blocks = jnp.where(same > 0, turned[:, g * 128 : (g + 1) * 128], 0.0)
        fore = blocks.T
        fore_ref[g * 128 : (g + 1) * 128, :] = fore
        for p in range(2):
            rows = slice(p * 64, (p + 1) * 64)
            plain = dot_exact(fore[rows, rows.start : rows.start + 64], spread[0:64, :], ((1,), (0,)))
            turn = dot_exact(
                blocks[rows, rows.start : rows.start + 64], spread_first[0:64, :], ((1,), (0,))
            )
            q = g * 2 + p
            for e in range(2):
                own = slice(e * 32, (e + 1) * 32)
                back_ref[q * 128 + e * 64 : q * 128 + e * 64 + 32, :] = plain[own, :]
                back_ref[q * 128 + e * 64 + 32 : q * 128 + e * 64 + 64, :] = turn[own, :]


def small_call(kernel, out_shape, *operands):
    return pl.pallas_call(
        kernel,
        out_shape=out_shape,
        compiler_params=pltpu.CompilerParams(vmem_limit_bytes=8 * 1024 * 1024),
    )(*operands)


def mix_maps(w_mix):
    return small_call(mix_maps_kernel, [f32(512, 128), f32(256, 128)], w_mix.T)


def own_mixing_rows(gram):
    point = lax.axis_index("point")
    odd = point // 4 % 2
    row = point // 8 * 128 + odd * 64 + point % 4 * 8
    rows = lax.dynamic_slice(gram, (row, odd * 64 + HEAD_SIZE), (8, HEAD_SIZE))
    return jnp.pad(rows, ((0, 0), (8, 88)))


def join_kernel(parts_ref, own_ref, out_ref):
    total = parts_ref[0]
    for k in range(1, 32):
        total = total + parts_ref[k]
    for k in range(8):
        out_ref[k, :, :] = total
        out_ref[k, :, 1024:1152] = total[:, 1024:1152] + own_ref[...]


def finish_kernel(parts_ref, value_ref, slice_ref, temp_ref, mix_ref, out_ref):
    total = parts_ref[0]
    for k in range(1, 8):
        total = total + parts_ref[k]
    value_ref[...] = total[:, 0:256]
    slice_ref[...] = total[:, 256:768]
    out_ref[...] = total[:, 768:1024]
    temp_ref[...] = total[:, 1024:1032]
    mix_ref[...] = total[:, 1032:1064]


def join(parts, own):
    return small_call(join_kernel, f32(8, 8, 1152), parts, own)


def finish(parts):
    shapes = [f32(8, 256), f32(8, 512), f32(8, 8), f32(8, 32), f32(8, 256)]
    return small_call(finish_kernel, shapes, parts)


def local(back_points, fore_points, cotangent, w_value, w_slice, w_temp, w_mix, w_out):
    fore_x = fore_points[0]
    back_x = back_points[0]
    cot = cotangent[0]
    turned_temp = w_temp.T

    sums, vo, stats, weights = back_sums(back_x, cot, w_slice, w_value, turned_temp, w_out)
    sums, turned_mix = tie(sums, w_mix)
    half = row_halves(sums)
    back_map, fore_map = mix_maps(turned_mix)
    half, back_map, fore = tie(half, back_map, jnp.zeros((144, 128), jnp.float32))
    half = quad_sum(half, along_x)
    fore, fore_wb = fore_sums(fore_x, weights, fore, None, 0, 1)
    half, fore = tie(half, fore)
    half = quad_sum(half, along_y)
    fore, fore_wb = fore_sums(fore_x, weights, fore, fore_wb, 1, 1)
    half, fore = tie(half, fore)
    sums = both_halves(half)
    fore_half = row_halves(fore)
    sums, fore_half = tie(sums, fore_half)
    fore_half = pair_sum(fore_half, along_x(1))

    wide, gram, stack = back_grads(sums, back_map, back_x, cot, weights, vo, stats)
    wide, gram, fore_half, turned_temp = tie(wide, gram, fore_half, turned_temp)
    parts = lax.all_to_all(wide.reshape(32, 8, 1152), "point", 0, 0)
    own_mix = own_mixing_rows(gram)
    fore_half = pair_sum(fore_half, along_x(3))
    grad_points = grad_of_points(stack, w_slice, w_value, turned_temp)
    fore_half, grad_points, own_mix = tie(fore_half, grad_points, own_mix)
    fore_half = pair_sum(fore_half, along_y(1))
    parts, fore_half = tie(parts, fore_half)
    parts = lax.all_to_all(join(parts, own_mix), "dp", 0, 0)
    fore = both_halves(pair_sum(fore_half, along_y(3)))
    fore_result = fore_results(fore, fore_map, fore_wb, w_out)
    parts, fore_result = tie(parts, fore_result)
    value_rows, slice_rows, temp_rows, mix_rows, out_rows = finish(parts)
    return (
        fore_result[None],
        grad_points[None],
        value_rows,
        slice_rows,
        temp_rows,
        mix_rows,
        out_rows,
    )


def solution(mesh):
    in_specs = (
        P("dp", "point", None),
        P("dp", "point", None),
        P("dp", "point", None),
        P(),
        P(),
        P(),
        P(),
        P(),
    )
    out_specs = (
        P("dp", "point", None),
        P("dp", "point", None),
        P("point", None),
        P("point", None),
        P("point", None),
        P("point", None),
        P("point", None),
    )
    return jax.shard_map(local, mesh=mesh, in_specs=in_specs, out_specs=out_specs, check_vma=False)
```

```python
import functools

import jax
import jax.numpy as jnp
from jax import lax
from jax.experimental import pallas as pl
from jax.experimental.pallas import tpu as pltpu
from jax.sharding import PartitionSpec as P

MODEL_WIDTH = 256
ATTENTION_HEADS = 8
HEAD_SIZE = 32
M = 64
TILE = 2048
FIRST_TILE = 1024
FIRST_SUB = 512
GRAD_TILE = 1024
SUB = 512
LOG2_E = 1.4426950408889634
VMEM_LIMIT = 20 * 1024 * 1024


epsilon = 1e-05

CORE_SWAP = [(i, i ^ 1) for i in range(32)]


def along_x(flip):
    return [(i, i ^ (8 * flip)) for i in range(32)]


def along_y(flip):
    return [(i, i ^ (2 * flip)) for i in range(32)]


def row_halves(flat, even):
    rows = flat.shape[0] // 2
    own = jnp.where(even, flat[:rows], flat[rows:])
    other = jnp.where(even, flat[rows:], flat[:rows])
    return own + lax.ppermute(other, "point", CORE_SWAP)


def pair_sum(half, pairs):
    return half + lax.ppermute(half, "point", pairs)


def quad_sum(half, pairs):
    parts = [lax.ppermute(half, "point", pairs(flip)) for flip in (1, 3, 2)]
    return half + parts[0] + parts[1] + parts[2]


def both_halves(half, even):
    other = lax.ppermute(half, "point", CORE_SWAP)
    return jnp.concatenate([jnp.where(even, half, other), jnp.where(even, other, half)])


def tie(*arrays):
    return lax.optimization_barrier(arrays)


def dot_nt(left, right):
    return lax.dot_general(
        left, right, (((1,), (1,)), ((), ())), preferred_element_type=jnp.float32
    )


def dot_nn(left, right):
    return jnp.dot(left, right, preferred_element_type=jnp.float32)


def dot_exact(left, right, dims):
    return lax.dot_general(
        left,
        right,
        ((dims, ((), ()))),
        precision=lax.Precision.HIGHEST,
        preferred_element_type=jnp.float32,
    )


def transpose_weights(wt, w_slice, w_value, w_temp):
    wt[0:512, :] = w_slice[...].T
    wt[512:768, :] = w_value[...].T
    wt[768:784, :] = padded_temp(w_temp).astype(jnp.bfloat16)


def padded_temp(w_temp):
    return jnp.concatenate(
        [w_temp[...].astype(jnp.float32), jnp.zeros((8, MODEL_WIDTH), jnp.float32)], axis=0
    )


def head_rows(h, size):
    return slice(h * size, (h + 1) * size)


def temper_of(coef):
    return 0.5 + jnp.maximum(coef, 0.0) + jnp.log1p(jnp.exp(-jnp.abs(coef)))


def lane_sum(w):
    total = w[:, 0:128]
    for k in range(1, w.shape[1] // 128):
        total = total + w[:, k * 128 : (k + 1) * 128]
    return total


def head_weights(logits, scale, wb, den, kept, h, columns, where=None):
    below = logits - jnp.max(logits, axis=0, keepdims=True)
    e = jnp.exp2(below * scale)
    inv = 1.0 / jnp.sum(e, axis=0, keepdims=True)
    w = e * inv
    wb[head_rows(h, M), columns] = w.astype(jnp.bfloat16)
    den[head_rows(h, M), :] += lane_sum(w)
    if kept is not None:
        kept[0][head_rows(h, M), where] = w
        kept[1][head_rows(h, M), where] = below


def pack_denominators(den):
    columns = [
        jnp.sum(den[head_rows(h, M), :], axis=1, keepdims=True) for h in range(ATTENTION_HEADS)
    ]
    lane = lax.broadcasted_iota(jnp.int32, (M, 128), 1)
    wide = jnp.zeros((M, 128), jnp.float32)
    for h in range(ATTENTION_HEADS):
        wide = jnp.where(lane == h, columns[h], wide)
    return jnp.concatenate(
        [wide.T[:8, :], jnp.zeros((8, M), jnp.float32)], axis=0
    )


def inverse_denominators(rows):
    tall = jnp.concatenate(
        [
            jnp.concatenate([rows, jnp.zeros((8, 128 - M), jnp.float32)], axis=1),
            jnp.zeros((120, 128), jnp.float32),
        ],
        axis=0,
    ).T
    inverse = 1.0 / (tall[:M, :] + epsilon)
    return [inverse[:, h : h + 1] for h in range(ATTENTION_HEADS)]


def back_sums_kernel(
    x_far, cot_far, ws_far, wv_far, wt_far, wo_far, fore_far,
    sums_ref, vo_ref, stats_ref, w_ref, below_ref, weights_ref, x_ref, cot_ref, fore_ref,
    wb, den, acc, ws, wv, wt, wo, sems,
):
    chunks = x_ref.shape[0] // FIRST_TILE

    def fetch(source, target, k):
        copy = pltpu.make_async_copy(source, target, sems.at[k])
        copy.start()
        return copy

    small = [fetch(a, b, k) for k, (a, b) in enumerate(
        [(ws_far, ws), (wv_far, wv), (wt_far, wt), (wo_far, wo)]
    )]
    large = []
    for c in range(chunks):
        rows = pl.ds(c * FIRST_TILE, FIRST_TILE)
        large.append((
            fetch(x_far.at[rows], x_ref.at[rows], 4 + 2 * c),
            fetch(cot_far.at[rows], cot_ref.at[rows], 5 + 2 * c),
        ))
    fore_copy = fetch(fore_far, fore_ref, 4 + 2 * chunks)
    den[...] = jnp.zeros_like(den)
    acc[...] = jnp.zeros_like(acc)
    for copy in small:
        copy.wait()
    transpose_weights(weights_ref, ws, wv, wt)
    for c in range(chunks):
        for copy in large[c]:
            copy.wait()
        for part in range(FIRST_TILE // FIRST_SUB):
            columns = slice(part * FIRST_SUB, (part + 1) * FIRST_SUB)
            where = slice(c * FIRST_TILE + part * FIRST_SUB, c * FIRST_TILE + (part + 1) * FIRST_SUB)
            projected = dot_nt(weights_ref[...], x_ref[where, :])
            values = projected[512:768, :].astype(jnp.bfloat16)
            out_grad = dot_nt(wo[...], cot_ref[where, :]).astype(jnp.bfloat16)
            coef = projected[768:776, :]
            inv_temper = 1.0 / temper_of(coef)
            stats_ref[0:8, where] = inv_temper
            stats_ref[8:16, where] = coef
            scale = inv_temper * LOG2_E
            for g in range(2):
                mixed_rows = []
                for j in range(4):
                    h = g * 4 + j
                    mixed_rows += [
                        values[head_rows(h, HEAD_SIZE), :], out_grad[head_rows(h, HEAD_SIZE), :]
                    ]
                    head_weights(
                        projected[head_rows(h, M), :], scale[h : h + 1, :], wb, den,
                        (w_ref, below_ref), h, columns, where,
                    )
                vo_ref[g * 256 : (g + 1) * 256, where] = jnp.concatenate(mixed_rows, axis=0)
        tile = slice(c * FIRST_TILE, (c + 1) * FIRST_TILE)
        for g in range(2):
            rows = slice(g * 256, (g + 1) * 256)
            acc[g, :, :] += dot_nt(wb[rows, :], vo_ref[rows, tile])

    lane = lax.broadcasted_iota(jnp.int32, (M, 128), 1)
    for q in range(4):
        g, p = q // 2, q % 2
        columns = slice(128 * p, 128 * p + 128)
        even = acc[g, 128 * p : 128 * p + 64, columns]
        odd = acc[g, 128 * p + 64 : 128 * p + 128, columns]
        sums_ref[q * M : (q + 1) * M, :] = jnp.where(lane < 64, even, odd)
    sums_ref[256:272, :] = jnp.zeros((16, 128), jnp.float32)
    sums_ref[256:272, 0:M] = pack_denominators(den)
    fore_copy.wait()


def fore_sums_kernel(x_ref, weights_ref, sums_ref, wb, den, acc, values):
    den[...] = jnp.zeros_like(den)
    acc[...] = jnp.zeros_like(acc)
    for c in range(x_ref.shape[0] // TILE):
        for part in range(TILE // SUB):
            columns = slice(part * SUB, (part + 1) * SUB)
            where = slice(c * TILE + part * SUB, c * TILE + (part + 1) * SUB)
            projected = dot_nt(weights_ref[...], x_ref[where, :])
            values[:, columns] = projected[512:768, :].astype(jnp.bfloat16)
            scale = LOG2_E / temper_of(projected[768:776, :])
            for h in range(ATTENTION_HEADS):
                head_weights(
                    projected[head_rows(h, M), :], scale[h : h + 1, :], wb, den, None, h, where
                )
        for g in range(2):
            acc[g, :, :] += dot_nt(
                wb[g * 256 : (g + 1) * 256, c * TILE : (c + 1) * TILE],
                values[g * 128 : (g + 1) * 128, :],
            )

    lane = lax.broadcasted_iota(jnp.int32, (M, 128), 1)
    for g in range(2):
        block = acc[g, 0:M, :]
        for j in range(1, 4):
            block = jnp.where(lane // HEAD_SIZE == j, acc[g, head_rows(j, M), :], block)
        sums_ref[g * M : (g + 1) * M, :] = block
    sums_ref[128:144, :] = jnp.zeros((16, 128), jnp.float32)
    sums_ref[128:144, 0:M] = pack_denominators(den)


def back_grads_kernel(
    sums_ref, mix_ref, x_ref, cot_ref, vo_ref, stats_ref, w_ref, below_ref, fore_wb,
    keep_ref, send_ref, stack_ref, fore_far,
    blocks, blocks_t, shift, wb, des, dots, grads, grad_out, wide, sem,
):
    step = pl.program_id(0)

    @pl.when(step == 0)
    def _():
        pltpu.make_async_copy(fore_wb, fore_far, sem).start()
        grads[...] = jnp.zeros_like(grads)
        grad_out[...] = jnp.zeros_like(grad_out)
        blocks[...] = jnp.zeros_like(blocks)
        lane = lax.broadcasted_iota(jnp.int32, (M, 128), 1)
        first = lane % 64 < HEAD_SIZE
        inverse = inverse_denominators(sums_ref[256:264, 0:M])
        for q in range(4):
            g, p = q // 2, q % 2
            scale = jnp.where(lane < 64, inverse[2 * q], inverse[2 * q + 1])
            scaled = sums_ref[q * M : (q + 1) * M, :] * jnp.where(first, scale, 1.0)
            mapped = dot_exact(scaled, mix_ref[q * 128 : (q + 1) * 128, :], ((1,), (0,)))
            product = jnp.where(first, mapped * scaled, 0.0)
            block = mapped * jnp.where(first, scale, 1.0)
            for e in range(2):
                h = 2 * q + e
                own = (lane // 64) == e
                rows = slice((h % 4) * M, (h % 4 + 1) * M)
                columns = slice(128 * p, 128 * p + 128)
                blocks[g, rows, columns] = jnp.where(own, block, 0.0).astype(jnp.bfloat16)
                gd = -jnp.sum(jnp.where(own, product, 0.0), axis=1, keepdims=True) * inverse[h]
                shift[head_rows(h, M), :] = jnp.broadcast_to(gd, (M, 128))
        for g in range(2):
            blocks_t[g, :, :] = blocks[g, :, :].T

    for part in range(GRAD_TILE // SUB):
        columns = slice(part * SUB, (part + 1) * SUB)
        where = pl.ds(pl.multiple_of(step * GRAD_TILE + part * SUB, SUB), SUB)
        for g in range(2):
            rows = slice(g * 256, (g + 1) * 256)
            grad_w = dot_nn(blocks[g, :, :], vo_ref[rows, where])
            for j in range(4):
                h = g * 4 + j
                w = w_ref[head_rows(h, M), where]
                wb[head_rows(h, M), columns] = w.astype(jnp.bfloat16)
                gd = shift[head_rows(h, M), :]
                gw = grad_w[head_rows(j, M), :] + jnp.concatenate([gd] * (SUB // 128), axis=1)
                inner = jnp.sum(w * gw, axis=0, keepdims=True)
                grad = w * ((gw - inner) * stats_ref[h : h + 1, where])
                dots[h : h + 1, columns] = jnp.sum(
                    grad * below_ref[head_rows(h, M), where], axis=0, keepdims=True
                )
                stack_ref[head_rows(h, M), columns] = grad.astype(jnp.bfloat16)
    for g in range(2):
        rows = slice(g * 256, (g + 1) * 256)
        both = dot_nn(blocks_t[g, :, :], wb[rows, :]).astype(jnp.bfloat16)
        for j in range(4):
            h = g * 4 + j
            stack_ref[512 + h * 32 : 544 + h * 32, :] = both[j * 64 : j * 64 + 32, :]
            des[head_rows(h, HEAD_SIZE), :] = both[j * 64 + 32 : j * 64 + 64, :]
    tile = pl.ds(pl.multiple_of(step * GRAD_TILE, GRAD_TILE), GRAD_TILE)
    grad_coef = -jax.nn.sigmoid(stats_ref[8:16, tile]) * dots[...] * stats_ref[0:8, tile]
    stack_ref[768:784, :] = jnp.concatenate(
        [grad_coef, jnp.zeros_like(grad_coef)], axis=0
    ).astype(jnp.bfloat16)
    grads[...] += dot_nn(stack_ref[...], x_ref[tile, :])
    grad_out[...] += dot_nn(des[...], cot_ref[tile, :])

    @pl.when(step == pl.num_programs(0) - 1)
    def _():
        wide[:, 0:256] = grads[512:768, :].T
        wide[:, 256:768] = grads[0:512, :].T
        wide[:, 768:1024] = grad_out[...]
        wide[:, 1024:1152] = jnp.concatenate(
            [grads[768:784, :], jnp.zeros((112, MODEL_WIDTH), jnp.float32)], axis=0
        ).T
        core = lax.rem(lax.axis_index("point"), 2)
        for chip in range(16):
            own = pl.multiple_of((chip * 2 + core) * 8, 8)
            other = pl.multiple_of((chip * 2 + 1 - core) * 8, 8)
            keep_ref[chip, :, :] = wide[pl.ds(own, 8), :]
            send_ref[chip, :, :] = wide[pl.ds(other, 8), :]
        pltpu.make_async_copy(fore_wb, fore_far, sem).wait()


def grad_points_kernel(stack_ref, ws_ref, wv_ref, wt_ref, out_ref, wide):
    @pl.when(pl.program_id(0) == 0)
    def _():
        wide[:, 0:512] = ws_ref[...]
        wide[:, 512:768] = wv_ref[...]
        wide[:, 768:784] = padded_temp(wt_ref).T.astype(jnp.bfloat16)

    out_ref[...] = dot_nn(wide[...], stack_ref[...]).T.astype(jnp.bfloat16)


def fore_result_kernel(sums_ref, mix_ref, wb_ref, wo_ref, out_ref, blocks_t, wo_t):
    @pl.when(pl.program_id(0) == 0)
    def _():
        wo_t[...] = wo_ref[...].T
        lane = lax.broadcasted_iota(jnp.int32, (M, 128), 1)
        inverse = inverse_denominators(sums_ref[128:136, 0:M])
        for g in range(2):
            scale = jnp.zeros((M, 128), jnp.float32)
            for j in range(4):
                scale = jnp.where(lane // HEAD_SIZE == j, inverse[g * 4 + j], scale)
            tokens = sums_ref[g * M : (g + 1) * M, :] * scale
            mixed = dot_exact(tokens, mix_ref[g * 128 : (g + 1) * 128, :], ((1,), (0,)))
            rows = [jnp.where(lane // HEAD_SIZE == j, mixed, 0.0) for j in range(4)]
            blocks_t[g, :, :] = jnp.concatenate(rows, axis=0).T.astype(jnp.bfloat16)

    parts = [
        dot_nn(blocks_t[g, :, :], wb_ref[g * 256 : (g + 1) * 256, :]).astype(jnp.bfloat16)
        for g in range(2)
    ]
    out = dot_nn(wo_t[...], jnp.concatenate(parts, axis=0))
    out_ref[...] = out.T.astype(jnp.bfloat16)


def f32(*shape):
    return jax.ShapeDtypeStruct(shape, jnp.float32)


def bf16(*shape):
    return jax.ShapeDtypeStruct(shape, jnp.bfloat16)


def near(*shape, dtype=jnp.bfloat16):
    return pltpu.VMEM(shape, dtype)


def rows_of(tile, width, first=0):
    return pl.BlockSpec((tile, width), lambda i: (i + first, 0))


def columns_of(tile, rows, first=0):
    return pl.BlockSpec((rows, tile), lambda i: (0, i + first))


def whole(*shape):
    return pl.BlockSpec(shape, lambda i: (0,) * len(shape))


NEAR = pl.BlockSpec(memory_space=pltpu.VMEM)


def call(kernel, points, tile, inputs, outputs, scratch, macs, moved, aliases={}):
    operands = [
        a if spec is NEAR else pltpu.with_memory_space_constraint(a, pltpu.HBM)
        for a, spec in inputs
    ]
    return pl.pallas_call(
        kernel,
        grid=(points // tile,),
        in_specs=[spec for _, spec in inputs],
        out_specs=[spec for _, spec in outputs],
        out_shape=[shape for shape, _ in outputs],
        scratch_shapes=scratch,
        input_output_aliases=aliases,
        compiler_params=pltpu.CompilerParams(vmem_limit_bytes=VMEM_LIMIT),
        cost_estimate=pl.CostEstimate(
            flops=2 * macs * points, bytes_accessed=moved * points, transcendentals=0
        ),
    )(*operands)


def back_sums(x, cot, w_slice, w_value, w_temp, w_out, fore_x):
    points = x.shape[0]
    operands = [
        pltpu.with_memory_space_constraint(a, pltpu.HBM)
        for a in (x, cot, w_slice, w_value, w_temp, w_out, fore_x)
    ]
    wide = functools.partial(near, dtype=jnp.float32)
    return pl.pallas_call(
        back_sums_kernel,
        in_specs=[pl.BlockSpec(memory_space=pltpu.HBM)] * 7,
        out_specs=[NEAR] * 9,
        out_shape=[
            f32(272, 128), near(512, points), wide(16, points), wide(512, points),
            wide(512, points), near(784, 256), near(points, 256), near(points, 256),
            near(points, 256),
        ],
        scratch_shapes=[
            pltpu.VMEM((512, FIRST_TILE), jnp.bfloat16), pltpu.VMEM((512, 128), jnp.float32),
            pltpu.VMEM((2, 256, 256), jnp.float32), pltpu.VMEM((256, 512), jnp.bfloat16),
            pltpu.VMEM((256, 256), jnp.bfloat16), pltpu.VMEM((8, 256), jnp.bfloat16),
            pltpu.VMEM((256, 256), jnp.bfloat16),
            pltpu.SemaphoreType.DMA((5 + 2 * (points // FIRST_TILE),)),
        ],
        compiler_params=pltpu.CompilerParams(vmem_limit_bytes=VMEM_LIMIT),
        cost_estimate=pl.CostEstimate(
            flops=1_200_000 * points, bytes_accessed=2200 * points, transcendentals=0
        ),
    )(*operands)


def fore_sums(x, weights):
    points = x.shape[0]
    return pl.pallas_call(
        fore_sums_kernel,
        in_specs=[NEAR, NEAR],
        out_specs=[NEAR, NEAR],
        out_shape=[f32(144, 128), near(512, points)],
        scratch_shapes=[
            pltpu.VMEM((512, 128), jnp.float32), pltpu.VMEM((2, 256, 128), jnp.float32),
            pltpu.VMEM((256, TILE), jnp.bfloat16),
        ],
        compiler_params=pltpu.CompilerParams(vmem_limit_bytes=VMEM_LIMIT),
        cost_estimate=pl.CostEstimate(
            flops=1_000_000 * points, bytes_accessed=1500 * points, transcendentals=0
        ),
    )(x, weights)


def back_grads(sums, mix, x, cot, vo, stats, w, below, fore_wb):
    points = x.shape[0]
    tile = GRAD_TILE
    return call(
        back_grads_kernel,
        points,
        tile,
        [(sums, NEAR), (mix, NEAR), (x, NEAR), (cot, NEAR),
         (vo, NEAR), (stats, NEAR), (w, NEAR), (below, NEAR),
         (fore_wb, NEAR)],
        [(near(16, 8, 1152, dtype=jnp.float32), NEAR), (near(16, 8, 1152, dtype=jnp.float32), NEAR),
         (pltpu.HBM((784, points), jnp.bfloat16), columns_of(tile, 784)),
         (pltpu.HBM((512, points), jnp.bfloat16), pl.BlockSpec(memory_space=pltpu.HBM))],
        [pltpu.VMEM((2, 256, 256), jnp.bfloat16), pltpu.VMEM((2, 256, 256), jnp.bfloat16),
         pltpu.VMEM((512, 128), jnp.float32), pltpu.VMEM((512, tile), jnp.bfloat16),
         pltpu.VMEM((256, tile), jnp.bfloat16), pltpu.VMEM((8, tile), jnp.float32),
         pltpu.VMEM((784, 256), jnp.float32), pltpu.VMEM((256, 256), jnp.float32),
         pltpu.VMEM((256, 1152), jnp.float32), pltpu.SemaphoreType.DMA],
        800_000,
        3800,
    )


def grad_of_points(stack, w_slice, w_value, w_temp):
    points = stack.shape[1]
    return call(
        grad_points_kernel,
        points,
        TILE,
        [(stack, columns_of(TILE, 784)), (w_slice, whole(256, 512)), (w_value, whole(256, 256)),
         (w_temp, whole(8, 256))],
        [(bf16(points, 256), rows_of(TILE, 256))],
        [pltpu.VMEM((256, 784), jnp.bfloat16)],
        200_000,
        2100,
    )[0]


def fore_results(sums, mix, wb, w_out):
    points = wb.shape[1]
    return call(
        fore_result_kernel,
        points,
        TILE,
        [(sums, NEAR), (mix, NEAR), (wb, columns_of(TILE, 512)), (w_out, whole(256, 256))],
        [(bf16(points, 256), rows_of(TILE, 256))],
        [pltpu.VMEM((2, 128, 256), jnp.bfloat16), pltpu.VMEM((256, 256), jnp.bfloat16)],
        130_000,
        1600,
    )[0]


def one_hot(rows, columns, hit):
    r = lax.broadcasted_iota(jnp.int32, (rows, columns), 0)
    c = lax.broadcasted_iota(jnp.int32, (rows, columns), 1)
    return jnp.where(hit(r, c), 1.0, 0.0)


def mix_maps_kernel(turned_ref, back_ref, fore_ref):
    turned = jnp.concatenate([turned_ref[...]] * 4, axis=0)
    spread = one_hot(128, 128, lambda r, c: (r // 32 == c // 64) & (r % 32 + 32 == c % 64))
    spread_first = one_hot(128, 128, lambda r, c: (r // 32 == c // 64) & (r % 32 == c % 64))
    same = one_hot(128, 128, lambda r, c: r // 32 == c // 32)
    for g in range(2):
        blocks = jnp.where(same > 0, turned[:, g * 128 : (g + 1) * 128], 0.0)
        fore = blocks.T
        fore_ref[g * 128 : (g + 1) * 128, :] = fore
        for p in range(2):
            rows = slice(p * 64, (p + 1) * 64)
            plain = dot_exact(fore[rows, rows.start : rows.start + 64], spread[0:64, :], ((1,), (0,)))
            turn = dot_exact(
                blocks[rows, rows.start : rows.start + 64], spread_first[0:64, :], ((1,), (0,))
            )
            q = g * 2 + p
            for e in range(2):
                own = slice(e * 32, (e + 1) * 32)
                back_ref[q * 128 + e * 64 : q * 128 + e * 64 + 32, :] = plain[own, :]
                back_ref[q * 128 + e * 64 + 32 : q * 128 + e * 64 + 64, :] = turn[own, :]


def small_call(kernel, out_shape, *operands):
    return pl.pallas_call(
        kernel,
        out_shape=out_shape,
        compiler_params=pltpu.CompilerParams(vmem_limit_bytes=8 * 1024 * 1024),
    )(*operands)


def mix_maps(w_mix):
    return small_call(mix_maps_kernel, [f32(512, 128), f32(256, 128)], w_mix.T)


def gram_kernel(sums_ref, gram_ref):
    lane = lax.broadcasted_iota(jnp.int32, (M, 128), 1)
    first = lane % 64 < HEAD_SIZE
    inverse = inverse_denominators(sums_ref[256:264, 0:M])
    for q in range(4):
        scale = jnp.where(lane < 64, inverse[2 * q], inverse[2 * q + 1])
        scaled = sums_ref[q * M : (q + 1) * M, :] * jnp.where(first, scale, 1.0)
        gram_ref[q * 128 : (q + 1) * 128, :] = dot_exact(scaled, scaled, ((0,), (0,)))


def own_mixing_rows(gram):
    point = lax.axis_index("point")
    odd = point // 4 % 2
    row = point // 8 * 128 + odd * 64 + point % 4 * 8
    rows = lax.dynamic_slice(gram, (row, odd * 64 + HEAD_SIZE), (8, HEAD_SIZE))
    return jnp.pad(rows, ((0, 0), (8, 88)))


def join_kernel(parts_ref, own_ref, out_ref):
    total = parts_ref[0]
    for k in range(1, 16):
        total = total + parts_ref[k]
    for k in range(8):
        out_ref[k, :, :] = total
        out_ref[k, :, 1024:1152] = total[:, 1024:1152] + own_ref[...]


def finish_kernel(parts_ref, value_ref, slice_ref, temp_ref, mix_ref, out_ref):
    total = parts_ref[0]
    for k in range(1, 8):
        total = total + parts_ref[k]
    value_ref[...] = total[:, 0:256]
    slice_ref[...] = total[:, 256:768]
    out_ref[...] = total[:, 768:1024]
    temp_ref[...] = total[:, 1024:1032]
    mix_ref[...] = total[:, 1032:1064]


def join(parts, own):
    return small_call(join_kernel, f32(8, 8, 1152), parts, own)


def finish(parts):
    shapes = [f32(8, 256), f32(8, 512), f32(8, 8), f32(8, 32), f32(8, 256)]
    return small_call(finish_kernel, shapes, parts)


def local(back_points, fore_points, cotangent, w_value, w_slice, w_temp, w_mix, w_out):
    fore_x = fore_points[0]
    back_x = back_points[0]
    cot = cotangent[0]
    even = lax.axis_index("point") % 2 == 0
    turned_temp, even = tie(w_temp.T, even)

    sums, vo, stats, w, below, weights, near_x, near_cot, near_fore = back_sums(
        back_x, cot, w_slice, w_value, turned_temp, w_out, fore_x
    )
    sums, turned_mix = tie(sums, w_mix)
    half = row_halves(sums, even)
    back_map, fore_map = mix_maps(turned_mix)
    half, back_map, weights = tie(half, back_map, weights)
    half = quad_sum(half, along_x)
    fore, fore_wb = fore_sums(near_fore, weights)
    half, fore = tie(half, fore)
    half = quad_sum(half, along_y)
    fore = pair_sum(pair_sum(fore, CORE_SWAP), along_x(1))
    half, fore = tie(half, fore)
    sums = both_halves(half, even)
    received = lax.ppermute(fore, "point", along_x(3))

    keep, send, stack, fore_wb = back_grads(
        sums, back_map, near_x, near_cot, vo, stats, w, below, fore_wb
    )
    send, sums, received, turned_temp = tie(send, sums, received, turned_temp)
    fore = fore + received
    blocks = keep + lax.ppermute(send, "point", CORE_SWAP)
    chips = [[i for i in range(32) if i % 2 == core] for core in range(2)]
    parts = lax.all_to_all(blocks, "point", 0, 0, axis_index_groups=chips)
    own_mix = own_mixing_rows(small_call(gram_kernel, f32(512, 128), sums))
    fore = pair_sum(fore, along_y(1))
    grad_points = grad_of_points(stack, w_slice, w_value, turned_temp)
    fore, grad_points, own_mix, parts = tie(fore, grad_points, own_mix, parts)
    received = lax.ppermute(fore, "point", along_y(3))
    joined = join(parts, own_mix)
    parts = lax.all_to_all(joined, "dp", 0, 0)
    joined, received = tie(joined, received)
    fore_result = fore_results(fore + received, fore_map, fore_wb, w_out)
    parts, fore_result = tie(parts, fore_result)
    value_rows, slice_rows, temp_rows, mix_rows, out_rows = finish(parts)
    return (
        fore_result[None],
        grad_points[None],
        value_rows,
        slice_rows,
        temp_rows,
        mix_rows,
        out_rows,
    )


def solution(mesh):
    in_specs = (
        P("dp", "point", None),
        P("dp", "point", None),
        P("dp", "point", None),
        P(),
        P(),
        P(),
        P(),
        P(),
    )
    out_specs = (
        P("dp", "point", None),
        P("dp", "point", None),
        P("point", None),
        P("point", None),
        P("point", None),
        P("point", None),
        P("point", None),
    )
    return jax.shard_map(local, mesh=mesh, in_specs=in_specs, out_specs=out_specs, check_vma=False)
```

```python
import functools

import jax
import jax.numpy as jnp
from jax import lax
from jax.experimental import pallas as pl
from jax.experimental.pallas import tpu as pltpu
from jax.sharding import PartitionSpec as P

MODEL_WIDTH = 256
ATTENTION_HEADS = 8
HEAD_SIZE = 32
M = 64
TILE = 2048
FIRST_TILE = 1024
FIRST_SUB = 512
GRAD_TILE = 1024
SUB = 512
LOG2_E = 1.4426950408889634
VMEM_LIMIT = 20 * 1024 * 1024


epsilon = 1e-05

CORE_SWAP = [(i, i ^ 1) for i in range(32)]


def along_x(flip):
    return [(i, i ^ (8 * flip)) for i in range(32)]


def along_y(flip):
    return [(i, i ^ (2 * flip)) for i in range(32)]


def row_halves(flat, even):
    rows = flat.shape[0] // 2
    own = jnp.where(even, flat[:rows], flat[rows:])
    other = jnp.where(even, flat[rows:], flat[:rows])
    return own + lax.ppermute(other, "point", CORE_SWAP)


def pair_sum(half, pairs):
    return half + lax.ppermute(half, "point", pairs)


def quad_sum(half, pairs):
    parts = [lax.ppermute(half, "point", pairs(flip)) for flip in (1, 3, 2)]
    return half + parts[0] + parts[1] + parts[2]


def both_halves(half, even):
    other = lax.ppermute(half, "point", CORE_SWAP)
    return jnp.concatenate([jnp.where(even, half, other), jnp.where(even, other, half)])


def tie(*arrays):
    return lax.optimization_barrier(arrays)


def dot_nt(left, right):
    return lax.dot_general(
        left, right, (((1,), (1,)), ((), ())), preferred_element_type=jnp.float32
    )


def dot_nn(left, right):
    return jnp.dot(left, right, preferred_element_type=jnp.float32)


def dot_exact(left, right, dims):
    return lax.dot_general(
        left,
        right,
        ((dims, ((), ()))),
        precision=lax.Precision.HIGHEST,
        preferred_element_type=jnp.float32,
    )


def transpose_weights(wt, w_slice, w_value, w_temp):
    wt[0:512, :] = w_slice[...].T
    wt[512:768, :] = w_value[...].T
    wt[768:784, :] = padded_temp(w_temp).astype(jnp.bfloat16)


def padded_temp(w_temp):
    return jnp.concatenate(
        [w_temp[...].astype(jnp.float32), jnp.zeros((8, MODEL_WIDTH), jnp.float32)], axis=0
    )


def head_rows(h, size):
    return slice(h * size, (h + 1) * size)


def temper_of(coef):
    return 0.5 + jnp.maximum(coef, 0.0) + jnp.log1p(jnp.exp(-jnp.abs(coef)))


def lane_sum(w):
    total = w[:, 0:128]
    for k in range(1, w.shape[1] // 128):
        total = total + w[:, k * 128 : (k + 1) * 128]
    return total


def head_weights(logits, scale, wb, den, kept, h, columns, where=None):
    below = logits - jnp.max(logits, axis=0, keepdims=True)
    e = jnp.exp2(below * scale)
    inv = 1.0 / jnp.sum(e, axis=0, keepdims=True)
    w = e * inv
    wb[head_rows(h, M), columns] = w.astype(jnp.bfloat16)
    den[head_rows(h, M), :] += lane_sum(w)
    if kept is not None:
        kept[0][head_rows(h, M), where] = w
        kept[1][head_rows(h, M), where] = below


def pack_denominators(den):
    columns = [
        jnp.sum(den[head_rows(h, M), :], axis=1, keepdims=True) for h in range(ATTENTION_HEADS)
    ]
    lane = lax.broadcasted_iota(jnp.int32, (M, 128), 1)
    wide = jnp.zeros((M, 128), jnp.float32)
    for h in range(ATTENTION_HEADS):
        wide = jnp.where(lane == h, columns[h], wide)
    return jnp.concatenate(
        [wide.T[:8, :], jnp.zeros((8, M), jnp.float32)], axis=0
    )


def inverse_denominators(rows):
    tall = jnp.concatenate(
        [
            jnp.concatenate([rows, jnp.zeros((8, 128 - M), jnp.float32)], axis=1),
            jnp.zeros((120, 128), jnp.float32),
        ],
        axis=0,
    ).T
    inverse = 1.0 / (tall[:M, :] + epsilon)
    return [inverse[:, h : h + 1] for h in range(ATTENTION_HEADS)]


def back_sums_kernel(
    x_far, cot_far, ws_far, wv_far, wt_far, wo_far, fore_far,
    sums_ref, vo_ref, stats_ref, w_ref, below_ref, weights_ref, x_ref, cot_ref, fore_ref,
    wb, den, acc, ws, wv, wt, wo, sems,
):
    chunks = x_ref.shape[0] // FIRST_TILE

    def fetch(source, target, k):
        copy = pltpu.make_async_copy(source, target, sems.at[k])
        copy.start()
        return copy

    small = [fetch(a, b, k) for k, (a, b) in enumerate(
        [(ws_far, ws), (wv_far, wv), (wt_far, wt), (wo_far, wo)]
    )]
    large = []
    for c in range(chunks):
        rows = pl.ds(c * FIRST_TILE, FIRST_TILE)
        large.append((
            fetch(x_far.at[rows], x_ref.at[rows], 4 + 2 * c),
            fetch(cot_far.at[rows], cot_ref.at[rows], 5 + 2 * c),
        ))
    fore_copy = fetch(fore_far, fore_ref, 4 + 2 * chunks)
    den[...] = jnp.zeros_like(den)
    acc[...] = jnp.zeros_like(acc)
    for copy in small:
        copy.wait()
    transpose_weights(weights_ref, ws, wv, wt)
    for c in range(chunks):
        for copy in large[c]:
            copy.wait()
        for part in range(FIRST_TILE // FIRST_SUB):
            columns = slice(part * FIRST_SUB, (part + 1) * FIRST_SUB)
            where = slice(c * FIRST_TILE + part * FIRST_SUB, c * FIRST_TILE + (part + 1) * FIRST_SUB)
            projected = dot_nt(weights_ref[...], x_ref[where, :])
            values = projected[512:768, :].astype(jnp.bfloat16)
            out_grad = dot_nt(wo[...], cot_ref[where, :]).astype(jnp.bfloat16)
            coef = projected[768:776, :]
            inv_temper = 1.0 / temper_of(coef)
            stats_ref[0:8, where] = inv_temper
            stats_ref[8:16, where] = coef
            scale = inv_temper * LOG2_E
            for g in range(2):
                mixed_rows = []
                for j in range(4):
                    h = g * 4 + j
                    mixed_rows += [
                        values[head_rows(h, HEAD_SIZE), :], out_grad[head_rows(h, HEAD_SIZE), :]
                    ]
                    head_weights(
                        projected[head_rows(h, M), :], scale[h : h + 1, :], wb, den,
                        (w_ref, below_ref), h, columns, where,
                    )
                vo_ref[g * 256 : (g + 1) * 256, where] = jnp.concatenate(mixed_rows, axis=0)
        tile = slice(c * FIRST_TILE, (c + 1) * FIRST_TILE)
        for g in range(2):
            rows = slice(g * 256, (g + 1) * 256)
            acc[g, :, :] += dot_nt(wb[rows, :], vo_ref[rows, tile])

    lane = lax.broadcasted_iota(jnp.int32, (M, 128), 1)
    for q in range(4):
        g, p = q // 2, q % 2
        columns = slice(128 * p, 128 * p + 128)
        even = acc[g, 128 * p : 128 * p + 64, columns]
        odd = acc[g, 128 * p + 64 : 128 * p + 128, columns]
        sums_ref[q * M : (q + 1) * M, :] = jnp.where(lane < 64, even, odd)
    sums_ref[256:272, :] = jnp.zeros((16, 128), jnp.float32)
    sums_ref[256:272, 0:M] = pack_denominators(den)
    fore_copy.wait()


def fore_sums_kernel(x_ref, weights_ref, sums_ref, wb, den, acc, values):
    den[...] = jnp.zeros_like(den)
    acc[...] = jnp.zeros_like(acc)
    for c in range(x_ref.shape[0] // TILE):
        for part in range(TILE // SUB):
            columns = slice(part * SUB, (part + 1) * SUB)
            where = slice(c * TILE + part * SUB, c * TILE + (part + 1) * SUB)
            projected = dot_nt(weights_ref[...], x_ref[where, :])
            values[:, columns] = projected[512:768, :].astype(jnp.bfloat16)
            scale = LOG2_E / temper_of(projected[768:776, :])
            for h in range(ATTENTION_HEADS):
                head_weights(
                    projected[head_rows(h, M), :], scale[h : h + 1, :], wb, den, None, h, where
                )
        for g in range(2):
            acc[g, :, :] += dot_nt(
                wb[g * 256 : (g + 1) * 256, c * TILE : (c + 1) * TILE],
                values[g * 128 : (g + 1) * 128, :],
            )

    lane = lax.broadcasted_iota(jnp.int32, (M, 128), 1)
    for g in range(2):
        block = acc[g, 0:M, :]
        for j in range(1, 4):
            block = jnp.where(lane // HEAD_SIZE == j, acc[g, head_rows(j, M), :], block)
        sums_ref[g * M : (g + 1) * M, :] = block
    sums_ref[128:144, :] = jnp.zeros((16, 128), jnp.float32)
    sums_ref[128:144, 0:M] = pack_denominators(den)


def back_grads_kernel(
    sums_ref, mix_ref, x_ref, cot_ref, vo_ref, stats_ref, w_ref, below_ref, fore_wb,
    keep_ref, send_ref, stack_ref, fore_far,
    blocks, blocks_t, shift, wb, des, dots, grads, grad_out, wide, sem,
):
    step = pl.program_id(0)

    @pl.when(step == 0)
    def _():
        pltpu.make_async_copy(fore_wb, fore_far, sem).start()
        grads[...] = jnp.zeros_like(grads)
        grad_out[...] = jnp.zeros_like(grad_out)
        blocks[...] = jnp.zeros_like(blocks)
        lane = lax.broadcasted_iota(jnp.int32, (M, 128), 1)
        first = lane % 64 < HEAD_SIZE
        inverse = inverse_denominators(sums_ref[256:264, 0:M])
        for q in range(4):
            g, p = q // 2, q % 2
            scale = jnp.where(lane < 64, inverse[2 * q], inverse[2 * q + 1])
            scaled = sums_ref[q * M : (q + 1) * M, :] * jnp.where(first, scale, 1.0)
            mapped = dot_exact(scaled, mix_ref[q * 128 : (q + 1) * 128, :], ((1,), (0,)))
            product = jnp.where(first, mapped * scaled, 0.0)
            block = mapped * jnp.where(first, scale, 1.0)
            for e in range(2):
                h = 2 * q + e
                own = (lane // 64) == e
                rows = slice((h % 4) * M, (h % 4 + 1) * M)
                columns = slice(128 * p, 128 * p + 128)
                blocks[g, rows, columns] = jnp.where(own, block, 0.0).astype(jnp.bfloat16)
                gd = -jnp.sum(jnp.where(own, product, 0.0), axis=1, keepdims=True) * inverse[h]
                shift[head_rows(h, M), :] = jnp.broadcast_to(gd, (M, 128))
        for g in range(2):
            blocks_t[g, :, :] = blocks[g, :, :].T

    for part in range(GRAD_TILE // SUB):
        columns = slice(part * SUB, (part + 1) * SUB)
        where = pl.ds(pl.multiple_of(step * GRAD_TILE + part * SUB, SUB), SUB)
        for g in range(2):
            rows = slice(g * 256, (g + 1) * 256)
            grad_w = dot_nn(blocks[g, :, :], vo_ref[rows, where])
            for j in range(4):
                h = g * 4 + j
                w = w_ref[head_rows(h, M), where]
                wb[head_rows(h, M), columns] = w.astype(jnp.bfloat16)
                gd = shift[head_rows(h, M), :]
                gw = grad_w[head_rows(j, M), :] + jnp.concatenate([gd] * (SUB // 128), axis=1)
                inner = jnp.sum(w * gw, axis=0, keepdims=True)
                grad = w * ((gw - inner) * stats_ref[h : h + 1, where])
                dots[h : h + 1, columns] = jnp.sum(
                    grad * below_ref[head_rows(h, M), where], axis=0, keepdims=True
                )
                stack_ref[head_rows(h, M), columns] = grad.astype(jnp.bfloat16)
    for g in range(2):
        rows = slice(g * 256, (g + 1) * 256)
        both = dot_nn(blocks_t[g, :, :], wb[rows, :]).astype(jnp.bfloat16)
        for j in range(4):
            h = g * 4 + j
            stack_ref[512 + h * 32 : 544 + h * 32, :] = both[j * 64 : j * 64 + 32, :]
            des[head_rows(h, HEAD_SIZE), :] = both[j * 64 + 32 : j * 64 + 64, :]
    tile = pl.ds(pl.multiple_of(step * GRAD_TILE, GRAD_TILE), GRAD_TILE)
    grad_coef = -jax.nn.sigmoid(stats_ref[8:16, tile]) * dots[...] * stats_ref[0:8, tile]
    stack_ref[768:784, :] = jnp.concatenate(
        [grad_coef, jnp.zeros_like(grad_coef)], axis=0
    ).astype(jnp.bfloat16)
    grads[...] += dot_nn(stack_ref[...], x_ref[tile, :])
    grad_out[...] += dot_nn(des[...], cot_ref[tile, :])

    @pl.when(step == pl.num_programs(0) - 1)
    def _():
        wide[:, 0:256] = grads[512:768, :].T
        wide[:, 256:768] = grads[0:512, :].T
        wide[:, 768:1024] = grad_out[...]
        wide[:, 1024:1152] = jnp.concatenate(
            [grads[768:784, :], jnp.zeros((112, MODEL_WIDTH), jnp.float32)], axis=0
        ).T
        core = lax.rem(lax.axis_index("point"), 2)
        for chip in range(16):
            own = pl.multiple_of((chip * 2 + core) * 8, 8)
            other = pl.multiple_of((chip * 2 + 1 - core) * 8, 8)
            keep_ref[chip, :, :] = wide[pl.ds(own, 8), :]
            send_ref[chip, :, :] = wide[pl.ds(other, 8), :]
        pltpu.make_async_copy(fore_wb, fore_far, sem).wait()


def grad_points_kernel(stack_ref, ws_ref, wv_ref, wt_ref, out_ref, wide):
    @pl.when(pl.program_id(0) == 0)
    def _():
        wide[:, 0:512] = ws_ref[...]
        wide[:, 512:768] = wv_ref[...]
        wide[:, 768:784] = padded_temp(wt_ref).T.astype(jnp.bfloat16)

    out_ref[...] = dot_nn(wide[...], stack_ref[...]).T.astype(jnp.bfloat16)


def fore_result_kernel(
    sums_ref, mix_ref, wb_far, wo_far, out_far, blocks_t, wo_t, wo, wb, out, sems
):
    def fetch(source, target, k):
        copy = pltpu.make_async_copy(source, target, sems.at[k])
        copy.start()
        return copy

    bounds = [0, TILE // 2, out.shape[0] - TILE // 2, out.shape[0]]
    tiles = [pl.ds(a, b - a) for a, b in zip(bounds, bounds[1:])]
    wo_copy = fetch(wo_far, wo, 0)
    arriving = [fetch(wb_far.at[:, t], wb.at[:, t], 1 + k) for k, t in enumerate(tiles)]
    lane = lax.broadcasted_iota(jnp.int32, (M, 128), 1)
    inverse = inverse_denominators(sums_ref[128:136, 0:M])
    for g in range(2):
        scale = jnp.zeros((M, 128), jnp.float32)
        for j in range(4):
            scale = jnp.where(lane // HEAD_SIZE == j, inverse[g * 4 + j], scale)
        tokens = sums_ref[g * M : (g + 1) * M, :] * scale
        mixed = dot_exact(tokens, mix_ref[g * 128 : (g + 1) * 128, :], ((1,), (0,)))
        rows = [jnp.where(lane // HEAD_SIZE == j, mixed, 0.0) for j in range(4)]
        blocks_t[g, :, :] = jnp.concatenate(rows, axis=0).T.astype(jnp.bfloat16)
    wo_copy.wait()
    wo_t[...] = wo[...].T
    leaving = []
    for k, t in enumerate(tiles):
        arriving[k].wait()
        parts = [
            dot_nn(blocks_t[g, :, :], wb[g * 256 : (g + 1) * 256, t]).astype(jnp.bfloat16)
            for g in range(2)
        ]
        product = dot_nn(wo_t[...], jnp.concatenate(parts, axis=0))
        out[t, :] = product.T.astype(jnp.bfloat16)
        leaving.append(fetch(out.at[t], out_far.at[t], 4 + k))
    for copy in leaving:
        copy.wait()


def f32(*shape):
    return jax.ShapeDtypeStruct(shape, jnp.float32)


def bf16(*shape):
    return jax.ShapeDtypeStruct(shape, jnp.bfloat16)


def near(*shape, dtype=jnp.bfloat16):
    return pltpu.VMEM(shape, dtype)


def rows_of(tile, width, first=0):
    return pl.BlockSpec((tile, width), lambda i: (i + first, 0))


def columns_of(tile, rows, first=0):
    return pl.BlockSpec((rows, tile), lambda i: (0, i + first))


def whole(*shape):
    return pl.BlockSpec(shape, lambda i: (0,) * len(shape))


NEAR = pl.BlockSpec(memory_space=pltpu.VMEM)


def call(kernel, points, tile, inputs, outputs, scratch, macs, moved, aliases={}):
    operands = [
        a if spec is NEAR else pltpu.with_memory_space_constraint(a, pltpu.HBM)
        for a, spec in inputs
    ]
    return pl.pallas_call(
        kernel,
        grid=(points // tile,),
        in_specs=[spec for _, spec in inputs],
        out_specs=[spec for _, spec in outputs],
        out_shape=[shape for shape, _ in outputs],
        scratch_shapes=scratch,
        input_output_aliases=aliases,
        compiler_params=pltpu.CompilerParams(vmem_limit_bytes=VMEM_LIMIT),
        cost_estimate=pl.CostEstimate(
            flops=2 * macs * points, bytes_accessed=moved * points, transcendentals=0
        ),
    )(*operands)


def back_sums(x, cot, w_slice, w_value, w_temp, w_out, fore_x):
    points = x.shape[0]
    operands = [
        pltpu.with_memory_space_constraint(a, pltpu.HBM)
        for a in (x, cot, w_slice, w_value, w_temp, w_out, fore_x)
    ]
    wide = functools.partial(near, dtype=jnp.float32)
    return pl.pallas_call(
        back_sums_kernel,
        in_specs=[pl.BlockSpec(memory_space=pltpu.HBM)] * 7,
        out_specs=[NEAR] * 9,
        out_shape=[
            f32(272, 128), near(512, points), wide(16, points), wide(512, points),
            wide(512, points), near(784, 256), near(points, 256), near(points, 256),
            near(points, 256),
        ],
        scratch_shapes=[
            pltpu.VMEM((512, FIRST_TILE), jnp.bfloat16), pltpu.VMEM((512, 128), jnp.float32),
            pltpu.VMEM((2, 256, 256), jnp.float32), pltpu.VMEM((256, 512), jnp.bfloat16),
            pltpu.VMEM((256, 256), jnp.bfloat16), pltpu.VMEM((8, 256), jnp.bfloat16),
            pltpu.VMEM((256, 256), jnp.bfloat16),
            pltpu.SemaphoreType.DMA((5 + 2 * (points // FIRST_TILE),)),
        ],
        compiler_params=pltpu.CompilerParams(vmem_limit_bytes=VMEM_LIMIT),
        cost_estimate=pl.CostEstimate(
            flops=1_200_000 * points, bytes_accessed=2200 * points, transcendentals=0
        ),
    )(*operands)


def fore_sums(x, weights):
    points = x.shape[0]
    return pl.pallas_call(
        fore_sums_kernel,
        in_specs=[NEAR, NEAR],
        out_specs=[NEAR, NEAR],
        out_shape=[f32(144, 128), near(512, points)],
        scratch_shapes=[
            pltpu.VMEM((512, 128), jnp.float32), pltpu.VMEM((2, 256, 128), jnp.float32),
            pltpu.VMEM((256, TILE), jnp.bfloat16),
        ],
        compiler_params=pltpu.CompilerParams(vmem_limit_bytes=VMEM_LIMIT),
        cost_estimate=pl.CostEstimate(
            flops=1_000_000 * points, bytes_accessed=1500 * points, transcendentals=0
        ),
    )(x, weights)


def back_grads(sums, mix, x, cot, vo, stats, w, below, fore_wb):
    points = x.shape[0]
    tile = GRAD_TILE
    return call(
        back_grads_kernel,
        points,
        tile,
        [(sums, NEAR), (mix, NEAR), (x, NEAR), (cot, NEAR),
         (vo, NEAR), (stats, NEAR), (w, NEAR), (below, NEAR),
         (fore_wb, NEAR)],
        [(near(16, 8, 1152, dtype=jnp.float32), NEAR), (near(16, 8, 1152, dtype=jnp.float32), NEAR),
         (pltpu.HBM((784, points), jnp.bfloat16), columns_of(tile, 784)),
         (pltpu.HBM((512, points), jnp.bfloat16), pl.BlockSpec(memory_space=pltpu.HBM))],
        [pltpu.VMEM((2, 256, 256), jnp.bfloat16), pltpu.VMEM((2, 256, 256), jnp.bfloat16),
         pltpu.VMEM((512, 128), jnp.float32), pltpu.VMEM((512, tile), jnp.bfloat16),
         pltpu.VMEM((256, tile), jnp.bfloat16), pltpu.VMEM((8, tile), jnp.float32),
         pltpu.VMEM((784, 256), jnp.float32), pltpu.VMEM((256, 256), jnp.float32),
         pltpu.VMEM((256, 1152), jnp.float32), pltpu.SemaphoreType.DMA],
        800_000,
        3800,
    )


def grad_of_points(stack, w_slice, w_value, w_temp):
    points = stack.shape[1]
    return call(
        grad_points_kernel,
        points,
        TILE,
        [(stack, columns_of(TILE, 784)), (w_slice, whole(256, 512)), (w_value, whole(256, 256)),
         (w_temp, whole(8, 256))],
        [(bf16(points, 256), rows_of(TILE, 256))],
        [pltpu.VMEM((256, 784), jnp.bfloat16)],
        200_000,
        2100,
    )[0]


def fore_results(sums, mix, wb, w_out):
    points = wb.shape[1]
    far = pl.BlockSpec(memory_space=pltpu.HBM)
    return pl.pallas_call(
        fore_result_kernel,
        in_specs=[NEAR, NEAR, far, far],
        out_specs=far,
        out_shape=pltpu.HBM((points, 256), jnp.bfloat16),
        scratch_shapes=[
            pltpu.VMEM((2, 128, 256), jnp.bfloat16), pltpu.VMEM((256, 256), jnp.bfloat16),
            pltpu.VMEM((256, 256), jnp.bfloat16), pltpu.VMEM((512, points), jnp.bfloat16),
            pltpu.VMEM((points, 256), jnp.bfloat16), pltpu.SemaphoreType.DMA((7,)),
        ],
        compiler_params=pltpu.CompilerParams(vmem_limit_bytes=VMEM_LIMIT),
        cost_estimate=pl.CostEstimate(
            flops=260_000 * points, bytes_accessed=1600 * points, transcendentals=0
        ),
    )(sums, mix, *(pltpu.with_memory_space_constraint(a, pltpu.HBM) for a in (wb, w_out)))


def one_hot(rows, columns, hit):
    r = lax.broadcasted_iota(jnp.int32, (rows, columns), 0)
    c = lax.broadcasted_iota(jnp.int32, (rows, columns), 1)
    return jnp.where(hit(r, c), 1.0, 0.0)


def mix_maps_kernel(turned_ref, back_ref, fore_ref):
    turned = jnp.concatenate([turned_ref[...]] * 4, axis=0)
    spread = one_hot(128, 128, lambda r, c: (r // 32 == c // 64) & (r % 32 + 32 == c % 64))
    spread_first = one_hot(128, 128, lambda r, c: (r // 32 == c // 64) & (r % 32 == c % 64))
    same = one_hot(128, 128, lambda r, c: r // 32 == c // 32)
    for g in range(2):
        blocks = jnp.where(same > 0, turned[:, g * 128 : (g + 1) * 128], 0.0)
        fore = blocks.T
        fore_ref[g * 128 : (g + 1) * 128, :] = fore
        for p in range(2):
            rows = slice(p * 64, (p + 1) * 64)
            plain = dot_exact(fore[rows, rows.start : rows.start + 64], spread[0:64, :], ((1,), (0,)))
            turn = dot_exact(
                blocks[rows, rows.start : rows.start + 64], spread_first[0:64, :], ((1,), (0,))
            )
            q = g * 2 + p
            for e in range(2):
                own = slice(e * 32, (e + 1) * 32)
                back_ref[q * 128 + e * 64 : q * 128 + e * 64 + 32, :] = plain[own, :]
                back_ref[q * 128 + e * 64 + 32 : q * 128 + e * 64 + 64, :] = turn[own, :]


def small_call(kernel, out_shape, *operands):
    return pl.pallas_call(
        kernel,
        out_shape=out_shape,
        compiler_params=pltpu.CompilerParams(vmem_limit_bytes=8 * 1024 * 1024),
    )(*operands)


def mix_maps(w_mix):
    return small_call(mix_maps_kernel, [f32(512, 128), f32(256, 128)], w_mix.T)


def gram_kernel(sums_ref, gram_ref):
    lane = lax.broadcasted_iota(jnp.int32, (M, 128), 1)
    first = lane % 64 < HEAD_SIZE
    inverse = inverse_denominators(sums_ref[256:264, 0:M])
    for q in range(4):
        scale = jnp.where(lane < 64, inverse[2 * q], inverse[2 * q + 1])
        scaled = sums_ref[q * M : (q + 1) * M, :] * jnp.where(first, scale, 1.0)
        gram_ref[q * 128 : (q + 1) * 128, :] = dot_exact(scaled, scaled, ((0,), (0,)))


def own_mixing_rows(gram):
    point = lax.axis_index("point")
    odd = point // 4 % 2
    row = point // 8 * 128 + odd * 64 + point % 4 * 8
    rows = lax.dynamic_slice(gram, (row, odd * 64 + HEAD_SIZE), (8, HEAD_SIZE))
    return jnp.pad(rows, ((0, 0), (8, 88)))


def join_kernel(parts_ref, own_ref, out_ref):
    total = parts_ref[0]
    for k in range(1, 16):
        total = total + parts_ref[k]
    for k in range(8):
        out_ref[k, :, :] = total
        out_ref[k, :, 1024:1152] = total[:, 1024:1152] + own_ref[...]


def finish_kernel(parts_ref, value_ref, slice_ref, temp_ref, mix_ref, out_ref):
    total = parts_ref[0]
    for k in range(1, 8):
        total = total + parts_ref[k]
    value_ref[...] = total[:, 0:256]
    slice_ref[...] = total[:, 256:768]
    out_ref[...] = total[:, 768:1024]
    temp_ref[...] = total[:, 1024:1032]
    mix_ref[...] = total[:, 1032:1064]


def join(parts, own):
    return small_call(join_kernel, f32(8, 8, 1152), parts, own)


def finish(parts):
    shapes = [f32(8, 256), f32(8, 512), f32(8, 8), f32(8, 32), f32(8, 256)]
    return small_call(finish_kernel, shapes, parts)


def local(back_points, fore_points, cotangent, w_value, w_slice, w_temp, w_mix, w_out):
    fore_x = fore_points[0]
    back_x = back_points[0]
    cot = cotangent[0]
    even = lax.axis_index("point") % 2 == 0
    turned_temp, even = tie(w_temp.T, even)

    sums, vo, stats, w, below, weights, near_x, near_cot, near_fore = back_sums(
        back_x, cot, w_slice, w_value, turned_temp, w_out, fore_x
    )
    sums, turned_mix = tie(sums, w_mix)
    half = row_halves(sums, even)
    back_map, fore_map = mix_maps(turned_mix)
    half, back_map, weights = tie(half, back_map, weights)
    half = quad_sum(half, along_x)
    fore, fore_wb = fore_sums(near_fore, weights)
    half, fore = tie(half, fore)
    half = quad_sum(half, along_y)
    fore = pair_sum(pair_sum(fore, CORE_SWAP), along_x(1))
    half, fore = tie(half, fore)
    sums = both_halves(half, even)
    received = lax.ppermute(fore, "point", along_x(3))

    keep, send, stack, fore_wb = back_grads(
        sums, back_map, near_x, near_cot, vo, stats, w, below, fore_wb
    )
    send, sums, received, turned_temp = tie(send, sums, received, turned_temp)
    fore = fore + received
    blocks = keep + lax.ppermute(send, "point", CORE_SWAP)
    chips = [[i for i in range(32) if i % 2 == core] for core in range(2)]
    parts = lax.all_to_all(blocks, "point", 0, 0, axis_index_groups=chips)
    own_mix = own_mixing_rows(small_call(gram_kernel, f32(512, 128), sums))
    fore = pair_sum(fore, along_y(1))
    grad_points = grad_of_points(stack, w_slice, w_value, turned_temp)
    fore, grad_points, own_mix, parts = tie(fore, grad_points, own_mix, parts)
    received = lax.ppermute(fore, "point", along_y(3))
    joined = join(parts, own_mix)
    parts = lax.all_to_all(joined, "dp", 0, 0)
    joined, received = tie(joined, received)
    fore_result = fore_results(fore + received, fore_map, fore_wb, w_out)
    parts, fore_result = tie(parts, fore_result)
    value_rows, slice_rows, temp_rows, mix_rows, out_rows = finish(parts)
    return (
        fore_result[None],
        grad_points[None],
        value_rows,
        slice_rows,
        temp_rows,
        mix_rows,
        out_rows,
    )


def solution(mesh):
    in_specs = (
        P("dp", "point", None),
        P("dp", "point", None),
        P("dp", "point", None),
        P(),
        P(),
        P(),
        P(),
        P(),
    )
    out_specs = (
        P("dp", "point", None),
        P("dp", "point", None),
        P("point", None),
        P("point", None),
        P("point", None),
        P("point", None),
        P("point", None),
    )
    return jax.shard_map(local, mesh=mesh, in_specs=in_specs, out_specs=out_specs, check_vma=False)
```
